32 devices in a mesh: occ: 2 (over x), vir: 16 (over z, y, core).
Axes of the slice: x: 2, y: 2, z: 4, core: 2. Of those that a mesh axis runs over, the one named last changes fastest.
Arguments:
- amplitudes: bfloat16 [1536, 2048], P('occ', 'vir'), may hold values from -6 to 6
- integrals: bfloat16 [2048, 40960], P('occ', 'vir'), may hold values from -0.375 to 0.375
- occ_sym: int32 [12], P('occ'), may hold values from 0 to 7, as said below
- vir_sym: int32 [320], P('vir'), may hold values from 0 to 7, as said below
- k_sym: int32 [16], replicated, may hold values from 0 to 7
Outputs:
- ladder: bfloat16 [1536, 40960], P('occ', 'vir')
The draws below stay inside these ranges and needn't reach their ends.
Inputs may be any that keep to these rules, and one draw needn't show every extreme that they name: `occ_sym`: among the 6 blocks of one index of occ no irrep occurs more than 2 times, and one occurs exactly 2 times. `vir_sym`: among the 20 blocks of one index of vir no irrep occurs more than 5 times, and one occurs exactly 5 times.
All inputs are finite; a program needn't handle non-finite values.
Results may differ from the reference program's by a relative error of at most 0.001.
Values may be sent and summed in bfloat16 or wider, within the bound.
No kernel may reach another device: no remote copies, remote signals or barrier semaphores. Data moves between devices by JAX's collectives and lax.ppermute only.
A program may use at most 64 MiB of HBM per device.

```python
import jax
import jax.numpy as jnp
from jax import lax

BLK = 128
IRREPS = 8
OCC_DEV = 768
VB_DEV = 20
KB = 16
MAXO = 2
MAXB = 5
OCC_PAIRS = 1536
VBLOCKS = 320
VPAIRS = 40960
KWIN = 2048
N_VIR = 16


def skewed_irreps(key, groups, group_size, slot_bound):
    group_keys = jax.random.split(key, groups)

    def per_group(group_key):
        first_key, second_key, third_key = jax.random.split(group_key, 3)
        hottest = jax.random.randint(first_key, (), 0, IRREPS)
        offset = jax.random.randint(second_key, (), 0, IRREPS - 1)
        places = jnp.arange(group_size, dtype=jnp.int32)
        others = (hottest + 1 + (offset + places - slot_bound) % (IRREPS - 1)) % IRREPS
        labels = jnp.where(places < slot_bound, hottest, others).astype(jnp.int32)
        return jax.random.permutation(third_key, labels)
    return jax.vmap(per_group)(group_keys).reshape(groups * group_size)


def draw_occ_sym(key, part):
    return skewed_irreps(key, OCC_PAIRS // OCC_DEV, OCC_DEV // BLK, MAXO)


def draw_vir_sym(key, part):
    return skewed_irreps(key, VBLOCKS // VB_DEV, VB_DEV, MAXB)


def touch_ends(values, own_key, low, top_value):
    longest = values.shape.index(max(values.shape))
    spots = []
    for shift in (0, 1):
        where = [jax.random.randint(jax.random.fold_in(own_key, axis), (), 0, length) for axis, length in enumerate(values.shape)]
        where[longest] = (where[longest] + shift) % values.shape[longest]
        spots.append(tuple(where))
    return values.at[spots[0]].set(low).at[spots[1]].set(top_value)


def shard_levels(key, shape, shards, smallest, high):
    gain, own = 1.0, jax.random.fold_in(key, 6)
    for dim, shards_of in shards:
        steps = jnp.exp(jax.random.uniform(jax.random.fold_in(own, dim), (shards_of,), jnp.float32, smallest / len(shards), high / len(shards)))
        gain = gain * jnp.repeat(steps, shape[dim] // shards_of).reshape([-1 if axis == dim else 1 for axis in range(len(shape))])
    return gain


def gaussian(own_key, dims, deviation, bound, cuts=(), kind=jnp.bfloat16):
    loudness = shard_levels(own_key, dims, cuts, -0.22, 0.18) if cuts else 1.0
    array = jax.random.normal(own_key, dims, jnp.float32) * deviation * loudness
    return jnp.minimum(jnp.maximum(array, -bound), bound).astype(kind)


def setup_inputs(seed: int = 0) -> dict:
    seeds = jax.random.split(jax.random.key(seed), 6)
    amplitudes = gaussian(seeds[0], (OCC_PAIRS, KWIN), 1.0, 6.0, ((0, 2), (1, 16)))
    integrals = gaussian(seeds[1], (KWIN, VPAIRS), (2 * BLK) ** -0.5, 0.375, ((0, 2), (1, 16)))
    occ_sym = draw_occ_sym(jax.random.fold_in(seeds[5], 71), 0)
    vir_sym = draw_vir_sym(jax.random.fold_in(seeds[5], 71), 0)
    k_sym = touch_ends(jax.random.randint(seeds[4], (KB,), 0, IRREPS), jax.random.fold_in(seeds[4], 1), 0, IRREPS - 1).astype(jnp.int32)
    return dict(amplitudes=amplitudes, integrals=integrals, occ_sym=occ_sym, vir_sym=vir_sym, k_sym=k_sym)


def slot_order(symmetry, labels, slot_bound):
    label_count = labels.shape[0]
    positions = jnp.arange(label_count, dtype=jnp.int32)
    matching = labels == symmetry
    ranking = jnp.where(matching, positions, positions + label_count)
    chosen = jnp.argsort(ranking)[:slot_bound].astype(jnp.int32)
    return chosen, matching[chosen]


def reference(amplitudes, integrals, occ_sym, vir_sym, k_sym):
    occ_blocks = occ_sym.shape[0]
    kblocks = k_sym.shape[0]
    allowed = (occ_sym[:, None] == k_sym[None, :]).astype(amplitudes.dtype)
    amp_masked = (amplitudes.reshape(occ_blocks, BLK, kblocks, BLK) * allowed[:, None, :, None]).reshape(OCC_PAIRS, KWIN)

    def one_span(device):
        device = device.astype(jnp.int32)
        labels = lax.dynamic_slice_in_dim(vir_sym, device * VB_DEV, VB_DEV)
        columns = lax.dynamic_slice_in_dim(integrals, device * (VB_DEV * BLK), VB_DEV * BLK, 1).reshape(KWIN, VB_DEV, BLK)

        def per_block(block_index, running):
            block_index = block_index.astype(jnp.int32)
            symmetry = k_sym[block_index]
            chosen, usable = slot_order(symmetry, labels, MAXB)
            block_rows = lax.dynamic_slice_in_dim(columns, block_index * BLK, BLK, 0)
            packed = block_rows[:, chosen, :] * usable[None, :, None].astype(block_rows.dtype)
            amp_cols = lax.dynamic_slice_in_dim(amp_masked, block_index * BLK, BLK, 1)
            product = jnp.dot(amp_cols, packed.reshape(BLK, MAXB * BLK), preferred_element_type=jnp.float32)
            return running.at[:, chosen, :].add(product.reshape(OCC_PAIRS, MAXB, BLK))

        summed = lax.fori_loop(0, kblocks, per_block, jnp.zeros((OCC_PAIRS, VB_DEV, BLK), jnp.float32))
        return summed.reshape(OCC_PAIRS, VB_DEV * BLK).astype(jnp.bfloat16)

    def fill(device, result):
        device = jnp.asarray(device).astype(jnp.int32)
        return lax.dynamic_update_slice_in_dim(result, one_span(device), device * (VB_DEV * BLK), 1)

    return lax.fori_loop(0, N_VIR, fill, jnp.zeros((OCC_PAIRS, VPAIRS), jnp.bfloat16))
```

```python
import functools

import jax
import jax.numpy as jnp
from jax import lax
from jax.experimental import pallas as pl
from jax.experimental.pallas import tpu as pltpu
from jax.sharding import PartitionSpec as P

BLK = 128
IRREPS = 8
MAXO = 2
MAXB = 5
INFO = 16

CNT = 0
VBL = CNT + IRREPS
SLOT = VBL + IRREPS * MAXB
OFF = SLOT + IRREPS * MAXO

SMEM = pl.BlockSpec(memory_space=pltpu.SMEM)
VMEM = pl.BlockSpec(memory_space=pltpu.VMEM)
ANY = pl.BlockSpec(memory_space=pl.ANY)
HBM = pl.BlockSpec(memory_space=pltpu.HBM)


def prep_kernel(
    n_occ, first_cap, ksym, vsym, osym, v_ref, a_ref, head, rest, pay, tab, sems
):
    kblocks, vblocks, oblocks = ksym.shape[0], vsym.shape[0], osym.shape[0]
    own = kblocks // n_occ
    first = lax.axis_index("occ") * own
    width = a_ref.shape[1]

    for s in range(IRREPS):
        tab[CNT + s] = 0
        for slot in range(MAXO):
            tab[SLOT + s * MAXO + slot] = -1

    @pl.loop(0, vblocks)
    def _(vb):
        s = vsym[vb]
        rank = tab[CNT + s]
        tab[VBL + s * MAXB + rank] = vb
        tab[CNT + s] = rank + 1

    most = jnp.int32(0)
    for half in range(n_occ):
        total = jnp.int32(0)
        for kb in range(half * own, (half + 1) * own):
            tab[OFF + kb] = total
            total = total + tab[CNT + ksym[kb]]
        most = jnp.maximum(most, total)

    def pieces(act):
        @pl.loop(0, own)
        def _(kb):
            s = ksym[first + kb]
            place0 = tab[OFF + first + kb]
            for j in range(MAXB):
                @pl.when(j < tab[CNT + s])
                def _():
                    place = place0 + j
                    src = v_ref.at[
                        pl.ds(pl.multiple_of(kb * BLK, BLK), BLK),
                        pl.ds(pl.multiple_of(tab[VBL + s * MAXB + j] * BLK, BLK), BLK),
                    ]

                    @pl.when(place < first_cap)
                    def _():
                        act(pltpu.make_async_copy(src, head.at[place], sems.at[place]))

                    @pl.when(place >= first_cap)
                    def _():
                        act(
                            pltpu.make_async_copy(
                                src, rest.at[place - first_cap], sems.at[place]
                            )
                        )

    pieces(lambda copy: copy.start())

    for ob in range(oblocks):
        s = osym[ob]
        used = (tab[SLOT + s * MAXO] >= 0).astype(jnp.int32)
        tab[SLOT + s * MAXO + used] = ob
    vir = lax.axis_index("vir")
    step = min(width, BLK)
    for q in range(width // step):
        s = ksym[(vir * width + q * step) // BLK]
        cols = slice(q * step, (q + 1) * step)
        for slot in range(MAXO):
            ob = tab[SLOT + s * MAXO + slot]
            rows = pl.ds(pl.multiple_of(jnp.maximum(ob, 0) * BLK, BLK), BLK)
            block = a_ref[rows, cols]
            pay[slot * BLK : (slot + 1) * BLK, cols] = jnp.where(
                ob >= 0, block, jnp.zeros_like(block)
            )
    pay[MAXO * BLK :, :] = jnp.full(
        (INFO, width), most.astype(jnp.float32), jnp.float32
    ).astype(jnp.bfloat16)

    pieces(lambda copy: copy.wait())


def add_half(first, own, ksym, tab, amp, read, acc, spare):
    @pl.loop(0, own)
    def _(i):
        kb = first + i
        s = ksym[kb]
        count = tab[CNT + s]
        place = tab[OFF + kb]

        @pl.when((tab[SLOT + s * MAXO] >= 0) & (count > 0))
        def _():
            left = amp[kb, : MAXO * BLK, :]
            for j in range(MAXB):
                there = j < count
                right = read(jnp.where(there, place + j, place))
                vb = jnp.where(there, tab[VBL + s * MAXB + j], spare)
                acc[vb] += jnp.dot(left, right, preferred_element_type=jnp.float32)


def own_kernel(masks, n_occ, first_cap, ksym, tab, *refs):
    n = len(masks) if masks else 1
    parts, (head, rest, acc, amp, zero_out, most, zeros, sems, zsems) = refs[:n], refs[n:]
    kblocks = ksym.shape[0]
    own = kblocks // n_occ
    vblocks = acc.shape[0] - 1
    me = lax.axis_index("vir")

    def gather(act):
        if not masks:
            act(pltpu.make_async_copy(parts[0], amp, sems.at[0]))
            return
        for i, (mask, part) in enumerate(zip(masks, parts)):
            act(pltpu.make_async_copy(part, amp.at[me ^ mask], sems.at[i]))

    gather(lambda copy: copy.start())
    zeros[...] = jnp.zeros_like(zeros)
    strips = zero_out.shape[0] // BLK

    def fill(act):
        for i in range(strips):
            act(
                pltpu.make_async_copy(
                    zeros, zero_out.at[pl.ds(i * BLK, BLK)], zsems.at[i]
                )
            )

    fill(lambda copy: copy.start())

    @pl.loop(0, vblocks)
    def _(vb):
        acc[vb] = jnp.zeros_like(acc[vb])

    gather(lambda copy: copy.wait())
    info = amp[:, MAXO * BLK : MAXO * BLK + INFO, :].astype(jnp.float32)
    most[0] = jnp.max(info).astype(jnp.int32)

    def read(place):
        return lax.cond(
            place < first_cap,
            lambda: head[jnp.minimum(place, first_cap - 1)],
            lambda: rest[jnp.maximum(place - first_cap, 0)],
        )

    add_half(
        lax.axis_index("occ") * own, own, ksym, tab, amp, read, acc, vblocks
    )
    fill(lambda copy: copy.wait())


def last_kernel(shifts, n_occ, first_cap, ksym, tab, amp, start, *refs):
    n = len(shifts)
    heads = refs[:n]
    rests = refs[n : 2 * n]
    _, out, acc, stage, sems = refs[-5:]
    kblocks = ksym.shape[0]
    own = kblocks // n_occ
    vblocks = acc.shape[0] - 1
    me = lax.axis_index("occ")

    @pl.loop(0, vblocks)
    def _(vb):
        acc[vb] = start[vb]

    for shift, head, rest in zip(shifts, heads, rests):
        source = lax.rem(me - shift + n_occ, n_occ)

        def read(place):
            return lax.cond(
                place < first_cap,
                lambda: head[jnp.minimum(place, first_cap - 1)],
                lambda: rest[jnp.maximum(place - first_cap, 0)],
            )

        add_half(source * own, own, ksym, tab, amp, read, acc, vblocks)

    def blocks(act):
        @pl.loop(0, IRREPS)
        def _(s):
            for slot in range(MAXO):
                ob = tab[SLOT + s * MAXO + slot]
                for j in range(MAXB):
                    @pl.when((ob >= 0) & (j < tab[CNT + s]))
                    def _():
                        act(ob, slot, tab[VBL + s * MAXB + j])

    def send(ob, slot, vb):
        return pltpu.make_async_copy(
            stage.at[vb, pl.ds(slot * BLK, BLK)],
            out.at[
                pl.ds(pl.multiple_of(ob * BLK, BLK), BLK),
                pl.ds(pl.multiple_of(vb * BLK, BLK), BLK),
            ],
            sems.at[vb, slot],
        )

    def store(ob, slot, vb):
        rows = slice(slot * BLK, (slot + 1) * BLK)
        stage[vb, rows, :] = acc[vb, rows, :].astype(jnp.bfloat16)
        send(ob, slot, vb).start()

    blocks(store)
    blocks(lambda ob, slot, vb: send(ob, slot, vb).wait())


def per_device(n_occ, n_vir, amplitudes, integrals, occ_sym, vir_sym, k_sym):
    occ_rows, width = amplitudes.shape
    kblocks = k_sym.shape[0]
    own = kblocks // n_occ
    vblocks = vir_sym.shape[0]
    cols = vblocks * BLK
    cap = own * MAXB
    first_cap = (cap * 3 + 3) // 4
    rows = MAXO * BLK + INFO
    bf16, f32, i32 = jnp.bfloat16, jnp.float32, jnp.int32

    head, rest, pay, tab = pl.pallas_call(
        functools.partial(prep_kernel, n_occ, first_cap),
        out_shape=(
            jax.ShapeDtypeStruct((first_cap, BLK, BLK), bf16),
            jax.ShapeDtypeStruct((cap - first_cap, BLK, BLK), bf16),
            jax.ShapeDtypeStruct((rows, width), bf16),
            jax.ShapeDtypeStruct((OFF + kblocks,), i32),
        ),
        in_specs=[SMEM, SMEM, SMEM, ANY, VMEM],
        out_specs=(VMEM, VMEM, VMEM, SMEM),
        scratch_shapes=[pltpu.SemaphoreType.DMA((cap,))],
        name="pack",
    )(k_sym, vir_sym, occ_sym, integrals, amplitudes)

    shifts = tuple(range(1, n_occ))

    def across(x, shift):
        return lax.ppermute(x, "occ", [(i, (i + shift) % n_occ) for i in range(n_occ)])

    heads = [across(head, shift) for shift in shifts]

    bits = [1 << b for b in range(n_vir.bit_length() - 1)]
    bits = bits[::-1]
    if width == BLK:
        parts, masks = [pay], [0]
        for bit in bits:
            pairs = [(i, i ^ bit) for i in range(n_vir)]
            parts = parts + [lax.ppermute(p, "vir", pairs) for p in parts]
            masks = masks + [m ^ bit for m in masks]
    else:
        whole, masks = pay[None], [0]
        for bit in bits:
            pairs = [(i, i ^ bit) for i in range(n_vir)]
            whole = jnp.concatenate([whole, lax.ppermute(whole, "vir", pairs)])
            masks = masks + [m ^ bit for m in masks]
        place = [masks.index(m) for m in range(n_vir)]
        order = jnp.asarray(place, i32)[
            jnp.arange(n_vir, dtype=i32) ^ lax.axis_index("vir").astype(i32)
        ]
        whole = whole[order].transpose(1, 0, 2).reshape(rows, kblocks, BLK)
        whole = whole.transpose(1, 0, 2)
        parts, masks = [whole], []
    acc, amp, zero_out, most = own_call(
        parts, masks, n_occ, first_cap, k_sym, tab, head, rest, kblocks, rows, vblocks,
        occ_rows, cols,
    )

    rests = lax.cond(
        most[0] > first_cap,
        lambda x: [across(x, shift) for shift in shifts],
        lambda x: [x for _ in shifts],
        rest,
    )
    return pl.pallas_call(
        functools.partial(last_kernel, shifts, n_occ, first_cap),
        out_shape=jax.ShapeDtypeStruct((occ_rows, cols), bf16),
        in_specs=[SMEM, SMEM] + [VMEM] * (2 + 2 * len(shifts)) + [HBM],
        out_specs=HBM,
        scratch_shapes=[
            pltpu.VMEM((vblocks + 1, MAXO * BLK, BLK), f32),
            pltpu.VMEM((vblocks, MAXO * BLK, BLK), bf16),
            pltpu.SemaphoreType.DMA((vblocks, MAXO)),
        ],
        input_output_aliases={4 + 2 * len(shifts): 0},
        compiler_params=pltpu.CompilerParams(vmem_limit_bytes=24 * 2**20),
        name="finish",
    )(k_sym, tab, amp, acc, *heads, *rests, zero_out)


def own_call(
    parts, masks, n_occ, first_cap, k_sym, tab, head, rest, kblocks, rows, vblocks,
    occ_rows, cols,
):
    bf16, f32, i32 = jnp.bfloat16, jnp.float32, jnp.int32
    return pl.pallas_call(
        functools.partial(own_kernel, tuple(masks), n_occ, first_cap),
        out_shape=(
            jax.ShapeDtypeStruct((vblocks + 1, MAXO * BLK, BLK), f32),
            jax.ShapeDtypeStruct((kblocks, rows, BLK), bf16),
            jax.ShapeDtypeStruct((occ_rows, cols), bf16),
            jax.ShapeDtypeStruct((1,), i32),
        ),
        in_specs=[SMEM, SMEM] + [ANY] * len(parts) + [VMEM, VMEM],
        out_specs=(VMEM, VMEM, HBM, SMEM),
        scratch_shapes=[
            pltpu.VMEM((BLK, cols), bf16),
            pltpu.SemaphoreType.DMA((len(parts),)),
            pltpu.SemaphoreType.DMA((occ_rows // BLK,)),
        ],
        compiler_params=pltpu.CompilerParams(vmem_limit_bytes=24 * 2**20),
        name="own_half",
    )(k_sym, tab, *parts, head, rest)


def solution(mesh):
    return jax.shard_map(
        functools.partial(per_device, mesh.shape["occ"], mesh.shape["vir"]),
        mesh=mesh,
        in_specs=(P("occ", "vir"), P("occ", "vir"), P("occ"), P("vir"), P()),
        out_specs=P("occ", "vir"),
        check_vma=False,
    )
```

```python
import functools

import jax
import jax.numpy as jnp
from jax import lax
from jax.experimental import pallas as pl
from jax.experimental.pallas import tpu as pltpu
from jax.sharding import PartitionSpec as P

BLK = 128
IRREPS = 8
MAXO = 2
MAXB = 5
INFO = 16

SMEM = pl.BlockSpec(memory_space=pltpu.SMEM)
VMEM = pl.BlockSpec(memory_space=pltpu.VMEM)
ANY = pl.BlockSpec(memory_space=pl.ANY)
HBM = pl.BlockSpec(memory_space=pltpu.HBM)


def here(x):
    return pltpu.with_memory_space_constraint(x, pltpu.VMEM)


def away(x):
    return pltpu.with_memory_space_constraint(x, pltpu.HBM)


class Table:
    def __init__(self, n_occ, kblocks, vblocks):
        self.n_occ, self.own, self.vblocks = n_occ, kblocks // n_occ, vblocks
        self.nk = 0
        self.kbl = self.nk + n_occ * IRREPS
        self.cnt = self.kbl + n_occ * IRREPS * self.own
        self.vbl = self.cnt + IRREPS
        self.slot = self.vbl + IRREPS * MAXB
        self.off = self.slot + IRREPS * MAXO
        self.total = self.off + n_occ * vblocks
        self.size = self.total + n_occ


def contraction_lists(t, ksym, tab):
    for i in range(t.n_occ * IRREPS):
        tab[t.nk + i] = 0
    for half in range(t.n_occ):
        for i in range(t.own):
            kb = half * t.own + i
            row = half * IRREPS + ksym[kb]
            rank = tab[t.nk + row]
            tab[t.kbl + row * t.own + rank] = kb
            tab[t.nk + row] = rank + 1


def pack_kernel(
    t, first_cap, ksym, vsym, osym, v_ref, a_ref, head, rest, pay, tab, sems
):
    own, vblocks, oblocks = t.own, t.vblocks, osym.shape[0]
    width = a_ref.shape[1]
    me = lax.axis_index("occ")
    others = tuple(lax.rem(me + d, t.n_occ) for d in range(1, t.n_occ))
    contraction_lists(t, ksym, tab)

    def block(row, rank, vb):
        kb = tab[t.kbl + row * own + rank] - me * own
        return v_ref.at[
            pl.ds(pl.multiple_of(kb * BLK, BLK), BLK),
            pl.ds(pl.multiple_of(vb * BLK, BLK), BLK),
        ]

    def send(vb, places):
        place0 = places[0]
        s = vsym[vb]
        row = me * IRREPS + s
        n = tab[t.nk + row]

        @pl.loop(0, n)
        def _(rank):
            place = place0 + rank

            @pl.when(place < first_cap)
            def _():
                pltpu.make_async_copy(
                    block(row, rank, vb), head.at[place], sems.at[place]
                ).start()

            @pl.when(place >= first_cap)
            def _():
                pltpu.make_async_copy(
                    block(row, rank, vb), rest.at[place - first_cap], sems.at[place]
                ).start()

        return (place0 + n,) + tuple(
            place + tab[t.nk + half * IRREPS + s]
            for half, place in zip(others, places[1:])
        )

    totals = lax.fori_loop(0, vblocks, send, (jnp.int32(0),) * t.n_occ)
    most = totals[0]
    for other in totals[1:]:
        most = jnp.maximum(most, other)

    vir = lax.axis_index("vir")
    step = min(width, BLK)
    for q in range(width // step):
        s = ksym[(vir * width + q * step) // BLK]
        cols = slice(q * step, (q + 1) * step)
        found = jnp.int32(0)
        slots = [jnp.int32(-1)] * MAXO
        for ob in range(oblocks):
            match = osym[ob] == s
            slots = [
                jnp.where(match & (found == i), ob, slot) for i, slot in enumerate(slots)
            ]
            found = found + match.astype(jnp.int32)
        for i, ob in enumerate(slots):
            rows = pl.ds(pl.multiple_of(jnp.maximum(ob, 0) * BLK, BLK), BLK)
            part = a_ref[rows, cols]
            pay[i * BLK : (i + 1) * BLK, cols] = jnp.where(
                ob >= 0, part, jnp.zeros_like(part)
            )
    pay[MAXO * BLK :, :] = jnp.full(
        (INFO, width), most.astype(jnp.float32), jnp.float32
    ).astype(jnp.bfloat16)

    @pl.loop(0, totals[0])
    def _(place):
        pltpu.make_async_copy(
            v_ref.at[pl.ds(0, BLK), pl.ds(0, BLK)], head.at[0], sems.at[place]
        ).wait()


def plan_kernel(t, ksym, vsym, osym, after, out, tab, *refs):
    del after
    zeros, sems = refs[-2:]
    zeros[...] = jnp.zeros_like(zeros)
    fills = [
        pltpu.make_async_copy(zeros, out.at[pl.ds(i * BLK, BLK)], sems.at[i])
        for i in range(out.shape[0] // BLK)
    ]
    for fill in fills:
        fill.start()

    contraction_lists(t, ksym, tab)
    for s in range(IRREPS):
        tab[t.cnt + s] = 0
        for slot in range(MAXO):
            tab[t.slot + s * MAXO + slot] = -1
    for ob in range(osym.shape[0]):
        s = osym[ob]
        used = (tab[t.slot + s * MAXO] >= 0).astype(jnp.int32)
        tab[t.slot + s * MAXO + used] = ob

    def count(vb, places):
        s = vsym[vb]
        rank = tab[t.cnt + s]
        tab[t.vbl + s * MAXB + rank] = vb
        tab[t.cnt + s] = rank + 1
        new = []
        for half, place in enumerate(places):
            tab[t.off + half * t.vblocks + vb] = place
            new.append(place + tab[t.nk + half * IRREPS + s])
        return tuple(new)

    totals = lax.fori_loop(0, t.vblocks, count, (jnp.int32(0),) * t.n_occ)
    for half, total in enumerate(totals):
        tab[t.total + half] = total
    for fill in fills:
        fill.wait()


def each_irrep(t, tab, spare, act):
    @pl.loop(0, IRREPS)
    def _(s):
        count = tab[t.cnt + s]
        vbs = [
            jnp.where(j < count, tab[t.vbl + s * MAXB + j], spare) for j in range(MAXB)
        ]
        one = tab[t.slot + s * MAXO] >= 0
        more = tab[t.slot + s * MAXO + 1] >= 0

        @pl.when((count > 0) & one & jnp.logical_not(more))
        def _():
            act(s, BLK, vbs)

        @pl.when((count > 0) & more)
        def _():
            act(s, MAXO * BLK, vbs)


def multiply(t, tab, half, s, rows, vbs, amp, blocks, acc, places):
    row = half * IRREPS + s
    offs = [
        jnp.where(
            vb < t.vblocks,
            tab[t.off + half * t.vblocks + jnp.minimum(vb, t.vblocks - 1)],
            0,
        )
        for vb in vbs
    ]

    @pl.loop(0, tab[t.nk + row])
    def _(rank):
        left = amp[tab[t.kbl + row * t.own + rank], :rows, :]
        for off, place in zip(offs, places):
            acc[place, :rows, :] += jnp.dot(
                left, blocks[off + rank], preferred_element_type=jnp.float32
            )


def sort_kernel(masks, *refs):
    parts, (amp, most) = refs[:-2], refs[-2:]
    peak = parts[0][..., MAXO * BLK :, :].astype(jnp.float32)
    if masks:
        me = lax.axis_index("vir")
        for mask, part in zip(masks, parts):
            amp[me ^ mask] = part[: MAXO * BLK, :]
            peak = jnp.maximum(peak, part[MAXO * BLK :, :].astype(jnp.float32))
    else:
        amp[...] = parts[0][:, : MAXO * BLK, :]
    most[0] = jnp.max(peak).astype(jnp.int32)


def finish_kernel(t, first_cap, tab, amp, *refs):
    n = t.n_occ
    heads, rests = refs[:n], refs[n : 2 * n]
    _, out, acc, stage, blocks, sems = refs[2 * n :]
    me = lax.axis_index("occ")
    halves = [lax.rem(me - shift + n, n) for shift in range(n)]

    def send(s, slot, vb):
        ob = tab[t.slot + s * MAXO + slot]
        return pltpu.make_async_copy(
            stage.at[vb, pl.ds(slot * BLK, BLK)],
            out.at[
                pl.ds(pl.multiple_of(ob * BLK, BLK), BLK),
                pl.ds(pl.multiple_of(vb * BLK, BLK), BLK),
            ],
            sems.at[vb, slot],
        )

    def products(sources):
        def act(s, rows, vbs):
            acc[:, :rows, :] = jnp.zeros((MAXB, rows, BLK), jnp.float32)
            for half, source in zip(halves, sources):
                multiply(t, tab, half, s, rows, vbs, amp, source, acc, range(MAXB))
            for j, vb in enumerate(vbs):

                @pl.when(vb < t.vblocks)
                def _():
                    stage[vb, :rows, :] = acc[j, :rows, :].astype(jnp.bfloat16)
                    for slot in range(rows // BLK):
                        send(s, slot, vb).start()

        each_irrep(t, tab, t.vblocks, act)

    most = tab[t.total]
    for half in range(1, n):
        most = jnp.maximum(most, tab[t.total + half])

    @pl.when(most <= first_cap)
    def _():
        products(heads)

    @pl.when(most > first_cap)
    def _():
        for i in range(n):
            blocks[i, :first_cap] = heads[i][...]
            pltpu.sync_copy(rests[i], blocks.at[i, pl.ds(first_cap, blocks.shape[1] - first_cap)])
        products([blocks.at[i] for i in range(n)])

    def settle(s, rows, vbs):
        for vb in vbs:

            @pl.when(vb < t.vblocks)
            def _():
                for slot in range(rows // BLK):
                    send(s, slot, vb).wait()

    each_irrep(t, tab, t.vblocks, settle)


def per_device(n_occ, n_vir, amplitudes, integrals, occ_sym, vir_sym, k_sym):
    occ_rows, width = amplitudes.shape
    kblocks = k_sym.shape[0]
    vblocks = vir_sym.shape[0]
    cols = vblocks * BLK
    t = Table(n_occ, kblocks, vblocks)
    cap = t.own * MAXB
    first_cap = (cap * 3 + 3) // 4
    rows = MAXO * BLK + INFO
    bf16, f32, i32 = jnp.bfloat16, jnp.float32, jnp.int32

    head, rest, pay = pl.pallas_call(
        functools.partial(pack_kernel, t, first_cap),
        out_shape=(
            pltpu.VMEM((first_cap, BLK, BLK), bf16),
            pltpu.VMEM((cap - first_cap, BLK, BLK), bf16),
            pltpu.VMEM((rows, width), bf16),
        ),
        in_specs=[SMEM, SMEM, SMEM, HBM, VMEM],
        out_specs=(VMEM, VMEM, VMEM),
        scratch_shapes=[
            pltpu.SMEM((t.size,), i32),
            pltpu.SemaphoreType.DMA((cap,)),
        ],
        compiler_params=pltpu.CompilerParams(vmem_limit_bytes=8 * 2**20),
        name="pack",
    )(*[away(x) for x in (k_sym, vir_sym, occ_sym, integrals, amplitudes)])
    zero_out, tab, *spares = pl.pallas_call(
        functools.partial(plan_kernel, t),
        out_shape=(pltpu.HBM((occ_rows, cols), bf16), pltpu.SMEM((t.size,), i32))
        + (pltpu.HBM((cap - first_cap, BLK, BLK), bf16),) * (n_occ - 1),
        in_specs=[SMEM, SMEM, SMEM, ANY],
        out_specs=(HBM, SMEM) + (HBM,) * (n_occ - 1),
        scratch_shapes=[
            pltpu.VMEM((BLK, cols), bf16),
            pltpu.SemaphoreType.DMA((occ_rows // BLK,)),
        ],
        compiler_params=pltpu.CompilerParams(vmem_limit_bytes=4 * 2**20),
        name="plan",
    )(*[away(x) for x in (k_sym, vir_sym, occ_sym)], pay)

    shifts = tuple(range(1, n_occ))

    def across(x, shift):
        return lax.ppermute(x, "occ", [(i, (i + shift) % n_occ) for i in range(n_occ)])

    heads = [across(head, shift) for shift in shifts]

    bits = [1 << b for b in range(n_vir.bit_length() - 1)][::-1]
    masks = [0]
    for bit in bits:
        masks = masks + [m ^ bit for m in masks]
    if width == BLK:
        parts = [pay]
        for bit in bits:
            pairs = [(i, i ^ bit) for i in range(n_vir)]
            parts = parts + [lax.ppermute(p, "vir", pairs) for p in parts]
            if len(parts) == 2:
                parts[1], zero_out = lax.optimization_barrier((parts[1], zero_out))
    else:
        whole = pay[None]
        for bit in bits:
            pairs = [(i, i ^ bit) for i in range(n_vir)]
            whole = jnp.concatenate([whole, lax.ppermute(whole, "vir", pairs)])
        place = [masks.index(m) for m in range(n_vir)]
        order = jnp.asarray(place, i32)[
            jnp.arange(n_vir, dtype=i32) ^ lax.axis_index("vir").astype(i32)
        ]
        whole = whole[order].transpose(1, 0, 2).reshape(rows, kblocks, BLK)
        parts, masks = [whole.transpose(1, 0, 2)], []

    amp, most = pl.pallas_call(
        functools.partial(sort_kernel, tuple(masks)),
        out_shape=(
            pltpu.VMEM((kblocks, MAXO * BLK, BLK), bf16),
            jax.ShapeDtypeStruct((1,), i32),
        ),
        in_specs=[VMEM] * len(parts),
        out_specs=(VMEM, SMEM),
        compiler_params=pltpu.CompilerParams(vmem_limit_bytes=8 * 2**20),
        name="sort",
    )(*parts)

    rests = lax.cond(
        most[0] > first_cap,
        lambda x, spares: [across(x, shift) for shift in shifts],
        lambda x, spares: spares,
        rest,
        spares,
    )
    heads, rests = [head] + heads, [rest] + rests
    return pl.pallas_call(
        functools.partial(finish_kernel, t, first_cap),
        out_shape=jax.ShapeDtypeStruct((occ_rows, cols), bf16),
        in_specs=[SMEM] + [VMEM] * (1 + n_occ) + [ANY] * n_occ + [HBM],
        out_specs=HBM,
        scratch_shapes=[
            pltpu.VMEM((MAXB, MAXO * BLK, BLK), f32),
            pltpu.VMEM((vblocks, MAXO * BLK, BLK), bf16),
            pltpu.VMEM((n_occ, cap, BLK, BLK), bf16),
            pltpu.SemaphoreType.DMA((vblocks, MAXO)),
        ],
        input_output_aliases={2 + 2 * n_occ: 0},
        compiler_params=pltpu.CompilerParams(vmem_limit_bytes=24 * 2**20),
        name="finish",
    )(tab, *[here(x) for x in (amp, *heads)], *rests, zero_out)


def solution(mesh):
    return jax.shard_map(
        functools.partial(per_device, mesh.shape["occ"], mesh.shape["vir"]),
        mesh=mesh,
        in_specs=(P("occ", "vir"), P("occ", "vir"), P("occ"), P("vir"), P()),
        out_specs=P("occ", "vir"),
        check_vma=False,
    )
```

```python
import functools

import jax
import jax.numpy as jnp
from jax import lax
from jax.experimental import pallas as pl
from jax.experimental.pallas import tpu as pltpu
from jax.sharding import PartitionSpec as P

BLK = 128
IRREPS = 8
MAXO = 2
MAXB = 5
INFO = 16

SMEM = pl.BlockSpec(memory_space=pltpu.SMEM)
VMEM = pl.BlockSpec(memory_space=pltpu.VMEM)
ANY = pl.BlockSpec(memory_space=pl.ANY)
HBM = pl.BlockSpec(memory_space=pltpu.HBM)


def here(x):
    return pltpu.with_memory_space_constraint(x, pltpu.VMEM)


def away(x):
    return pltpu.with_memory_space_constraint(x, pltpu.HBM)


class Table:
    def __init__(self, n_occ, kblocks, vblocks):
        self.n_occ, self.own, self.vblocks = n_occ, kblocks // n_occ, vblocks
        self.nk = 0
        self.kbl = self.nk + n_occ * IRREPS
        self.cnt = self.kbl + n_occ * IRREPS * self.own
        self.vbl = self.cnt + IRREPS
        self.slot = self.vbl + IRREPS * MAXB
        self.off = self.slot + IRREPS * MAXO
        self.total = self.off + n_occ * vblocks
        self.size = self.total + n_occ


def contraction_lists(t, ksym, tab, halves):
    for half in halves:
        for s in range(IRREPS):
            tab[t.nk + half * IRREPS + s] = 0
        for i in range(t.own):
            kb = half * t.own + i
            row = half * IRREPS + ksym[kb]
            rank = tab[t.nk + row]
            tab[t.kbl + row * t.own + rank] = kb
            tab[t.nk + row] = rank + 1


def pack_kernel(
    t, first_cap, ksym, vsym, osym, v_ref, a_ref, head, rest, pay, tab, sems
):
    own, vblocks, oblocks = t.own, t.vblocks, osym.shape[0]
    width = a_ref.shape[1]
    me = lax.axis_index("occ")
    others = tuple(lax.rem(me + d, t.n_occ) for d in range(1, t.n_occ))
    contraction_lists(t, ksym, tab, [me])

    def block(row, rank, vb):
        kb = tab[t.kbl + row * own + rank] - me * own
        return v_ref.at[
            pl.ds(pl.multiple_of(kb * BLK, BLK), BLK),
            pl.ds(pl.multiple_of(vb * BLK, BLK), BLK),
        ]

    total = jnp.int32(0)
    for vb in range(vblocks):
        row = me * IRREPS + vsym[vb]
        n = tab[t.nk + row]

        @pl.loop(0, n)
        def _(rank, vb=vb, row=row, place0=total):
            place = place0 + rank

            @pl.when(place < first_cap)
            def _():
                pltpu.make_async_copy(
                    block(row, rank, vb), head.at[place], sems.at[place]
                ).start()

            @pl.when(place >= first_cap)
            def _():
                pltpu.make_async_copy(
                    block(row, rank, vb), rest.at[place - first_cap], sems.at[place]
                ).start()

        total = total + n

    contraction_lists(t, ksym, tab, others)
    most = total
    for half in others:
        other = jnp.int32(0)
        for vb in range(vblocks):
            other = other + tab[t.nk + half * IRREPS + vsym[vb]]
        most = jnp.maximum(most, other)

    vir = lax.axis_index("vir")
    step = min(width, BLK)
    for q in range(width // step):
        s = ksym[(vir * width + q * step) // BLK]
        cols = slice(q * step, (q + 1) * step)
        found = jnp.int32(0)
        slots = [jnp.int32(-1)] * MAXO
        for ob in range(oblocks):
            match = osym[ob] == s
            slots = [
                jnp.where(match & (found == i), ob, slot) for i, slot in enumerate(slots)
            ]
            found = found + match.astype(jnp.int32)
        for i, ob in enumerate(slots):
            rows = pl.ds(pl.multiple_of(jnp.maximum(ob, 0) * BLK, BLK), BLK)
            part = a_ref[rows, cols]
            pay[i * BLK : (i + 1) * BLK, cols] = jnp.where(
                ob >= 0, part, jnp.zeros_like(part)
            )
    pay[MAXO * BLK :, :] = jnp.full(
        (INFO, width), most.astype(jnp.float32), jnp.float32
    ).astype(jnp.bfloat16)

    @pl.loop(0, total)
    def _(place):
        pltpu.make_async_copy(
            v_ref.at[pl.ds(0, BLK), pl.ds(0, BLK)], head.at[0], sems.at[place]
        ).wait()


def plan_kernel(t, ksym, vsym, osym, after, out, tab, *refs):
    del after
    zeros, sems = refs[-2:]
    zeros[...] = jnp.zeros_like(zeros)
    fills = [
        pltpu.make_async_copy(zeros, out.at[pl.ds(i * BLK, BLK)], sems.at[i])
        for i in range(out.shape[0] // BLK)
    ]
    for fill in fills:
        fill.start()

    contraction_lists(t, ksym, tab, range(t.n_occ))
    for s in range(IRREPS):
        tab[t.cnt + s] = 0
        for slot in range(MAXO):
            tab[t.slot + s * MAXO + slot] = -1
    for ob in range(osym.shape[0]):
        s = osym[ob]
        used = (tab[t.slot + s * MAXO] >= 0).astype(jnp.int32)
        tab[t.slot + s * MAXO + used] = ob

    def count(vb, places):
        s = vsym[vb]
        rank = tab[t.cnt + s]
        tab[t.vbl + s * MAXB + rank] = vb
        tab[t.cnt + s] = rank + 1
        new = []
        for half, place in enumerate(places):
            tab[t.off + half * t.vblocks + vb] = place
            new.append(place + tab[t.nk + half * IRREPS + s])
        return tuple(new)

    totals = lax.fori_loop(0, t.vblocks, count, (jnp.int32(0),) * t.n_occ)
    for half, total in enumerate(totals):
        tab[t.total + half] = total
    for fill in fills:
        fill.wait()


def each_irrep(t, tab, act, variants):
    @pl.loop(0, IRREPS)
    def _(s):
        count = tab[t.cnt + s]
        rows = jnp.where(tab[t.slot + s * MAXO] >= 0, BLK, 0)
        for slot in range(1, MAXO):
            more = tab[t.slot + s * MAXO + slot] >= 0
            rows = jnp.where(more, (slot + 1) * BLK, rows)
        todo = (count > 0) & (rows > 0)
        for have, width in variants:
            fits = todo & (rows <= have) & (count <= width)

            @pl.when(fits)
            def _():
                act(
                    s,
                    have,
                    [
                        jnp.where(j < count, tab[t.vbl + s * MAXB + j], -1)
                        for j in range(width)
                    ],
                )

            todo = todo & jnp.logical_not(fits)


def multiply(t, tab, halves, s, rows, vbs, amp, sources, acc):
    bases = [half * IRREPS + s for half in halves]
    counts = [tab[t.nk + row] for row in bases]
    offs = [
        [jnp.where(vb >= 0, tab[t.off + half * t.vblocks + jnp.maximum(vb, 0)], 0) for vb in vbs]
        for half in halves
    ]
    steps = counts[0]
    for count in counts[1:]:
        steps = jnp.maximum(steps, count)

    def terms(rank):
        sums = [None] * len(vbs)
        for row, count, places, source in zip(bases, counts, offs, sources):
            there = rank < count
            here = jnp.where(there, rank, 0)
            kb = jnp.where(there, tab[t.kbl + row * t.own + here], 0)
            left = amp[kb, :rows, :]
            for j, place in enumerate(places):
                part = jnp.dot(
                    left,
                    source[jnp.where(there, place + here, 0)],
                    preferred_element_type=jnp.float32,
                )
                part = jnp.where(there, part, 0.0)
                sums[j] = part if sums[j] is None else sums[j] + part
        return sums

    for j, part in enumerate(terms(jnp.int32(0))):
        acc[j, :rows, :] = part

    @pl.loop(1, steps)
    def _(rank):
        for j, part in enumerate(terms(rank)):
            acc[j, :rows, :] += part


def sort_kernel(masks, *refs):
    parts, (amp, most) = refs[:-2], refs[-2:]
    peak = parts[0][..., MAXO * BLK :, :].astype(jnp.float32)
    if masks:
        me = lax.axis_index("vir")
        for mask, part in zip(masks, parts):
            amp[me ^ mask] = part[: MAXO * BLK, :]
            peak = jnp.maximum(peak, part[MAXO * BLK :, :].astype(jnp.float32))
    else:
        amp[...] = parts[0][:, : MAXO * BLK, :]
    most[0] = jnp.max(peak).astype(jnp.int32)


def finish_kernel(t, first_cap, tab, amp, *refs):
    n = t.n_occ
    heads, rests = refs[:n], refs[n : 2 * n]
    _, out, acc, stage, blocks, sent, sems = refs[2 * n :]
    me = lax.axis_index("occ")
    halves = [lax.rem(me - shift + n, n) for shift in range(n)]

    sent[0] = 0

    def send(s, slot, vb, index):
        ob = tab[t.slot + s * MAXO + slot]
        return pltpu.make_async_copy(
            stage.at[vb, pl.ds(slot * BLK, BLK)],
            out.at[
                pl.ds(pl.multiple_of(ob * BLK, BLK), BLK),
                pl.ds(pl.multiple_of(vb * BLK, BLK), BLK),
            ],
            sems.at[index],
        )

    def store(s, slot, j, vb):
        rows = slice(slot * BLK, (slot + 1) * BLK)
        stage[vb, rows, :] = acc[j, rows, :].astype(jnp.bfloat16)
        index = sent[0]
        send(s, slot, vb, index).start()
        sent[0] = index + 1

    def products(sources, variants):
        def act(s, rows, vbs):
            multiply(t, tab, halves, s, rows, vbs, amp, sources, acc)
            for j, vb in enumerate(vbs):
                for slot in range(rows // BLK):

                    @pl.when((vb >= 0) & (tab[t.slot + s * MAXO + slot] >= 0))
                    def _():
                        store(s, slot, j, vb)

        each_irrep(t, tab, act, variants)

    whole = ((MAXO * BLK, MAXB),)
    usual = ((BLK, 2), (BLK, 3), (BLK, MAXB), (MAXO * BLK, 3)) + whole

    most = tab[t.total]
    for half in range(1, n):
        most = jnp.maximum(most, tab[t.total + half])

    @pl.when(most <= first_cap)
    def _():
        products(heads, usual)

    @pl.when(most > first_cap)
    def _():
        for i in range(n):
            blocks[i, :first_cap] = heads[i][...]
            pltpu.sync_copy(rests[i], blocks.at[i, pl.ds(first_cap, blocks.shape[1] - first_cap)])
        products([blocks.at[i] for i in range(n)], whole)

    @pl.loop(0, sent[0])
    def _(index):
        pltpu.make_async_copy(
            stage.at[0, pl.ds(0, BLK)],
            out.at[pl.ds(0, BLK), pl.ds(0, BLK)],
            sems.at[index],
        ).wait()


def per_device(n_occ, n_vir, amplitudes, integrals, occ_sym, vir_sym, k_sym):
    occ_rows, width = amplitudes.shape
    kblocks = k_sym.shape[0]
    vblocks = vir_sym.shape[0]
    cols = vblocks * BLK
    t = Table(n_occ, kblocks, vblocks)
    cap = t.own * MAXB
    first_cap = (cap * 3 + 3) // 4
    rows = MAXO * BLK + INFO
    bf16, f32, i32 = jnp.bfloat16, jnp.float32, jnp.int32

    head, rest, pay = pl.pallas_call(
        functools.partial(pack_kernel, t, first_cap),
        out_shape=(
            pltpu.VMEM((first_cap, BLK, BLK), bf16),
            pltpu.VMEM((cap - first_cap, BLK, BLK), bf16),
            pltpu.VMEM((rows, width), bf16),
        ),
        in_specs=[SMEM, SMEM, SMEM, HBM, VMEM],
        out_specs=(VMEM, VMEM, VMEM),
        scratch_shapes=[
            pltpu.SMEM((t.size,), i32),
            pltpu.SemaphoreType.DMA((cap,)),
        ],
        compiler_params=pltpu.CompilerParams(vmem_limit_bytes=8 * 2**20),
        name="pack",
    )(*[away(x) for x in (k_sym, vir_sym, occ_sym, integrals, amplitudes)])
    zero_out, tab, *spares = pl.pallas_call(
        functools.partial(plan_kernel, t),
        out_shape=(pltpu.HBM((occ_rows, cols), bf16), pltpu.SMEM((t.size,), i32))
        + (pltpu.HBM((cap - first_cap, BLK, BLK), bf16),) * (n_occ - 1),
        in_specs=[SMEM, SMEM, SMEM, ANY],
        out_specs=(HBM, SMEM) + (HBM,) * (n_occ - 1),
        scratch_shapes=[
            pltpu.VMEM((BLK, cols), bf16),
            pltpu.SemaphoreType.DMA((occ_rows // BLK,)),
        ],
        compiler_params=pltpu.CompilerParams(vmem_limit_bytes=4 * 2**20),
        name="plan",
    )(*[away(x) for x in (k_sym, vir_sym, occ_sym)], pay)

    shifts = tuple(range(1, n_occ))

    def across(x, shift):
        return lax.ppermute(x, "occ", [(i, (i + shift) % n_occ) for i in range(n_occ)])

    heads = [across(head, shift) for shift in shifts]

    bits = [1 << b for b in range(n_vir.bit_length() - 1)][::-1]
    masks = [0]
    for bit in bits:
        masks = masks + [m ^ bit for m in masks]
    if width == BLK:
        parts = [pay]
        for bit in bits:
            pairs = [(i, i ^ bit) for i in range(n_vir)]
            parts = parts + [lax.ppermute(p, "vir", pairs) for p in parts]
            if len(parts) == 2:
                parts[1], zero_out = lax.optimization_barrier((parts[1], zero_out))
    else:
        whole = pay[None]
        for bit in bits:
            pairs = [(i, i ^ bit) for i in range(n_vir)]
            whole = jnp.concatenate([whole, lax.ppermute(whole, "vir", pairs)])
        place = [masks.index(m) for m in range(n_vir)]
        order = jnp.asarray(place, i32)[
            jnp.arange(n_vir, dtype=i32) ^ lax.axis_index("vir").astype(i32)
        ]
        whole = whole[order].transpose(1, 0, 2).reshape(rows, kblocks, BLK)
        parts, masks = [whole.transpose(1, 0, 2)], []

    amp, most = pl.pallas_call(
        functools.partial(sort_kernel, tuple(masks)),
        out_shape=(
            pltpu.VMEM((kblocks, MAXO * BLK, BLK), bf16),
            jax.ShapeDtypeStruct((1,), i32),
        ),
        in_specs=[VMEM] * len(parts),
        out_specs=(VMEM, SMEM),
        compiler_params=pltpu.CompilerParams(vmem_limit_bytes=8 * 2**20),
        name="sort",
    )(*parts)

    rests = lax.cond(
        most[0] > first_cap,
        lambda x, spares: [across(x, shift) for shift in shifts],
        lambda x, spares: spares,
        rest,
        spares,
    )
    heads, rests = [head] + heads, [rest] + rests
    return pl.pallas_call(
        functools.partial(finish_kernel, t, first_cap),
        out_shape=jax.ShapeDtypeStruct((occ_rows, cols), bf16),
        in_specs=[SMEM] + [VMEM] * (1 + n_occ) + [ANY] * n_occ + [HBM],
        out_specs=HBM,
        scratch_shapes=[
            pltpu.VMEM((MAXB, MAXO * BLK, BLK), f32),
            pltpu.VMEM((vblocks, MAXO * BLK, BLK), bf16),
            pltpu.VMEM((n_occ, cap, BLK, BLK), bf16),
            pltpu.SMEM((1,), i32),
            pltpu.SemaphoreType.DMA((vblocks * MAXO,)),
        ],
        input_output_aliases={2 + 2 * n_occ: 0},
        compiler_params=pltpu.CompilerParams(vmem_limit_bytes=24 * 2**20),
        name="finish",
    )(tab, *[here(x) for x in (amp, *heads)], *rests, zero_out)


def solution(mesh):
    return jax.shard_map(
        functools.partial(per_device, mesh.shape["occ"], mesh.shape["vir"]),
        mesh=mesh,
        in_specs=(P("occ", "vir"), P("occ", "vir"), P("occ"), P("vir"), P()),
        out_specs=P("occ", "vir"),
        check_vma=False,
    )
```

```python
import functools

import jax
import jax.numpy as jnp
from jax import lax
from jax.experimental import pallas as pl
from jax.experimental.pallas import tpu as pltpu
from jax.sharding import PartitionSpec as P

BLK = 128
IRREPS = 8
MAXO = 2
MAXB = 5
INFO = 16

SMEM = pl.BlockSpec(memory_space=pltpu.SMEM)
VMEM = pl.BlockSpec(memory_space=pltpu.VMEM)
ANY = pl.BlockSpec(memory_space=pl.ANY)
HBM = pl.BlockSpec(memory_space=pltpu.HBM)


def here(x):
    return pltpu.with_memory_space_constraint(x, pltpu.VMEM)


def away(x):
    return pltpu.with_memory_space_constraint(x, pltpu.HBM)


class Table:
    def __init__(self, n_occ, kblocks, vblocks):
        self.n_occ, self.own, self.vblocks = n_occ, kblocks // n_occ, vblocks
        self.nk = 0
        self.kbl = self.nk + n_occ * IRREPS
        self.cnt = self.kbl + n_occ * IRREPS * self.own
        self.vbl = self.cnt + IRREPS
        self.slot = self.vbl + IRREPS * MAXB
        self.off = self.slot + IRREPS * MAXO
        self.total = self.off + n_occ * vblocks
        self.size = self.total + n_occ


def contraction_lists(t, ksym, tab, halves):
    for half in halves:
        for s in range(IRREPS):
            tab[t.nk + half * IRREPS + s] = 0
        for i in range(t.own):
            kb = half * t.own + i
            row = half * IRREPS + ksym[kb]
            rank = tab[t.nk + row]
            tab[t.kbl + row * t.own + rank] = kb
            tab[t.nk + row] = rank + 1


def pack_kernel(t, chunks, ksym, vsym, osym, v_ref, a_ref, *refs):
    packed, (pay, tab, sems) = refs[: len(chunks)], refs[len(chunks) :]
    own, vblocks, oblocks = t.own, t.vblocks, osym.shape[0]
    width = a_ref.shape[1]
    me = lax.axis_index("occ")
    others = tuple(lax.rem(me + d, t.n_occ) for d in range(1, t.n_occ))
    contraction_lists(t, ksym, tab, [me])

    def block(row, rank, vb):
        kb = tab[t.kbl + row * own + rank] - me * own
        return v_ref.at[
            pl.ds(pl.multiple_of(kb * BLK, BLK), BLK),
            pl.ds(pl.multiple_of(vb * BLK, BLK), BLK),
        ]

    total = jnp.int32(0)
    for vb in range(vblocks):
        row = me * IRREPS + vsym[vb]
        n = tab[t.nk + row]

        @pl.loop(0, n)
        def _(rank, vb=vb, row=row, place0=total):
            place = place0 + rank

            def start(chunk, place0):
                pltpu.make_async_copy(
                    block(row, rank, vb), chunk.at[place - place0], sems.at[place]
                ).start()

            @pl.when(place < chunks[0])
            def _():
                start(packed[0], 0)

            @pl.when(place >= chunks[0])
            def _():
                place0 = chunks[0]
                for size, chunk in zip(chunks[1:], packed[1:]):

                    @pl.when((place >= place0) & (place < place0 + size))
                    def _(chunk=chunk, place0=place0):
                        start(chunk, place0)

                    place0 += size

        total = total + n

    contraction_lists(t, ksym, tab, others)
    most = total
    for half in others:
        other = jnp.int32(0)
        for vb in range(vblocks):
            other = other + tab[t.nk + half * IRREPS + vsym[vb]]
        most = jnp.maximum(most, other)

    vir = lax.axis_index("vir")
    step = min(width, BLK)
    for q in range(width // step):
        s = ksym[(vir * width + q * step) // BLK]
        cols = slice(q * step, (q + 1) * step)
        found = jnp.int32(0)
        slots = [jnp.int32(-1)] * MAXO
        for ob in range(oblocks):
            match = osym[ob] == s
            slots = [
                jnp.where(match & (found == i), ob, slot) for i, slot in enumerate(slots)
            ]
            found = found + match.astype(jnp.int32)
        for i, ob in enumerate(slots):
            rows = pl.ds(pl.multiple_of(jnp.maximum(ob, 0) * BLK, BLK), BLK)
            part = a_ref[rows, cols]
            pay[i * BLK : (i + 1) * BLK, cols] = jnp.where(
                ob >= 0, part, jnp.zeros_like(part)
            )
    pay[MAXO * BLK :, :] = jnp.full(
        (INFO, width), most.astype(jnp.float32), jnp.float32
    ).astype(jnp.bfloat16)

    @pl.loop(0, total)
    def _(place):
        pltpu.make_async_copy(
            v_ref.at[pl.ds(0, BLK), pl.ds(0, BLK)], packed[0].at[0], sems.at[place]
        ).wait()


def plan_kernel(t, ksym, vsym, osym, after, out, tab, *refs):
    del after
    zeros, sems = refs[-2:]
    zeros[...] = jnp.zeros_like(zeros)
    fills = [
        pltpu.make_async_copy(zeros, out.at[pl.ds(i * BLK, BLK)], sems.at[i])
        for i in range(out.shape[0] // BLK)
    ]
    for fill in fills:
        fill.start()

    contraction_lists(t, ksym, tab, range(t.n_occ))
    for s in range(IRREPS):
        tab[t.cnt + s] = 0
        for slot in range(MAXO):
            tab[t.slot + s * MAXO + slot] = -1
    for ob in range(osym.shape[0]):
        s = osym[ob]
        used = (tab[t.slot + s * MAXO] >= 0).astype(jnp.int32)
        tab[t.slot + s * MAXO + used] = ob

    def count(vb, places):
        s = vsym[vb]
        rank = tab[t.cnt + s]
        tab[t.vbl + s * MAXB + rank] = vb
        tab[t.cnt + s] = rank + 1
        new = []
        for half, place in enumerate(places):
            tab[t.off + half * t.vblocks + vb] = place
            new.append(place + tab[t.nk + half * IRREPS + s])
        return tuple(new)

    totals = lax.fori_loop(0, t.vblocks, count, (jnp.int32(0),) * t.n_occ)
    for half, total in enumerate(totals):
        tab[t.total + half] = total
    for fill in fills:
        fill.wait()


def each_irrep(t, tab, act, variants):
    @pl.loop(0, IRREPS)
    def _(s):
        count = tab[t.cnt + s]
        rows = jnp.where(tab[t.slot + s * MAXO] >= 0, BLK, 0)
        for slot in range(1, MAXO):
            more = tab[t.slot + s * MAXO + slot] >= 0
            rows = jnp.where(more, (slot + 1) * BLK, rows)
        todo = (count > 0) & (rows > 0)
        for have, width in variants:
            fits = todo & (rows <= have) & (count <= width)

            @pl.when(fits)
            def _():
                act(
                    s,
                    have,
                    [
                        jnp.where(j < count, tab[t.vbl + s * MAXB + j], -1)
                        for j in range(width)
                    ],
                )

            todo = todo & jnp.logical_not(fits)


def multiply(t, tab, halves, s, rows, vbs, amp, sources, acc):
    bases = [half * IRREPS + s for half in halves]
    counts = [tab[t.nk + row] for row in bases]
    offs = [
        [jnp.where(vb >= 0, tab[t.off + half * t.vblocks + jnp.maximum(vb, 0)], 0) for vb in vbs]
        for half in halves
    ]
    steps = counts[0]
    for count in counts[1:]:
        steps = jnp.maximum(steps, count)

    def terms(rank):
        sums = [None] * len(vbs)
        for row, count, places, source in zip(bases, counts, offs, sources):
            there = rank < count
            here = jnp.where(there, rank, 0)
            kb = jnp.where(there, tab[t.kbl + row * t.own + here], 0)
            left = amp[kb, :rows, :]
            for j, place in enumerate(places):
                part = jnp.dot(
                    left,
                    source[jnp.where(there, place + here, 0)],
                    preferred_element_type=jnp.float32,
                )
                part = jnp.where(there, part, 0.0)
                sums[j] = part if sums[j] is None else sums[j] + part
        return sums

    for j, part in enumerate(terms(jnp.int32(0))):
        acc[j, :rows, :] = part

    @pl.loop(1, steps)
    def _(rank):
        for j, part in enumerate(terms(rank)):
            acc[j, :rows, :] += part


def sort_kernel(masks, *refs):
    parts, (amp, most) = refs[:-2], refs[-2:]
    peak = parts[0][..., MAXO * BLK :, :].astype(jnp.float32)
    if masks:
        me = lax.axis_index("vir")
        for mask, part in zip(masks, parts):
            amp[me ^ mask] = part[: MAXO * BLK, :]
            peak = jnp.maximum(peak, part[MAXO * BLK :, :].astype(jnp.float32))
    else:
        amp[...] = parts[0][:, : MAXO * BLK, :]
    most[0] = jnp.max(peak).astype(jnp.int32)


def finish_kernel(t, chunks, tab, amp, *refs):
    n = t.n_occ
    heads, rests = refs[:n], refs[n : n * len(chunks)]
    _, out, acc, stage, blocks, sent, sems, load_sems = refs[n * len(chunks) :]
    me = lax.axis_index("occ")
    halves = [lax.rem(me - shift + n, n) for shift in range(n)]

    sent[0] = 0

    def send(s, slot, vb, index):
        ob = tab[t.slot + s * MAXO + slot]
        return pltpu.make_async_copy(
            stage.at[vb, pl.ds(slot * BLK, BLK)],
            out.at[
                pl.ds(pl.multiple_of(ob * BLK, BLK), BLK),
                pl.ds(pl.multiple_of(vb * BLK, BLK), BLK),
            ],
            sems.at[index],
        )

    def store(s, slot, j, vb):
        rows = slice(slot * BLK, (slot + 1) * BLK)
        stage[vb, rows, :] = acc[j, rows, :].astype(jnp.bfloat16)
        index = sent[0]
        send(s, slot, vb, index).start()
        sent[0] = index + 1

    def products(sources, variants):
        def act(s, rows, vbs):
            multiply(t, tab, halves, s, rows, vbs, amp, sources, acc)
            for j, vb in enumerate(vbs):
                for slot in range(rows // BLK):

                    @pl.when((vb >= 0) & (tab[t.slot + s * MAXO + slot] >= 0))
                    def _():
                        store(s, slot, j, vb)

        each_irrep(t, tab, act, variants)

    whole = ((MAXO * BLK, MAXB),)
    usual = ((BLK, 2), (BLK, 3), (BLK, MAXB), (MAXO * BLK, 3)) + whole

    most = tab[t.total]
    for half in range(1, n):
        most = jnp.maximum(most, tab[t.total + half])

    @pl.when(most <= chunks[0])
    def _():
        products(heads, usual)

    @pl.when(most > chunks[0])
    def _():
        def load(act):
            place = chunks[0]
            for c, size in enumerate(chunks[1:]):

                @pl.when(most > place)
                def _(c=c, size=size, place=place):
                    for i in range(n):
                        act(
                            pltpu.make_async_copy(
                                rests[c * n + i],
                                blocks.at[i, pl.ds(place, size)],
                                load_sems.at[c * n + i],
                            )
                        )

                place += size

        load(lambda copy: copy.start())
        for i in range(n):
            blocks[i, : chunks[0]] = heads[i][...]
        load(lambda copy: copy.wait())
        products([blocks.at[i] for i in range(n)], usual)

    @pl.loop(0, sent[0])
    def _(index):
        pltpu.make_async_copy(
            stage.at[0, pl.ds(0, BLK)],
            out.at[pl.ds(0, BLK), pl.ds(0, BLK)],
            sems.at[index],
        ).wait()


def per_device(n_occ, n_vir, amplitudes, integrals, occ_sym, vir_sym, k_sym):
    occ_rows, width = amplitudes.shape
    kblocks = k_sym.shape[0]
    vblocks = vir_sym.shape[0]
    cols = vblocks * BLK
    t = Table(n_occ, kblocks, vblocks)
    cap = t.own * MAXB
    first_cap = (cap * 27 + 39) // 40
    more_cap = (cap - first_cap) // 3
    chunks = tuple(c for c in (first_cap, more_cap, cap - first_cap - more_cap) if c)
    rows = MAXO * BLK + INFO
    bf16, f32, i32 = jnp.bfloat16, jnp.float32, jnp.int32

    *packed, pay = pl.pallas_call(
        functools.partial(pack_kernel, t, chunks),
        out_shape=tuple(pltpu.VMEM((c, BLK, BLK), bf16) for c in chunks)
        + (pltpu.VMEM((rows, width), bf16),),
        in_specs=[SMEM, SMEM, SMEM, HBM, VMEM],
        out_specs=(VMEM,) * (len(chunks) + 1),
        scratch_shapes=[
            pltpu.SMEM((t.size,), i32),
            pltpu.SemaphoreType.DMA((cap,)),
        ],
        compiler_params=pltpu.CompilerParams(vmem_limit_bytes=8 * 2**20),
        name="pack",
    )(*[away(x) for x in (k_sym, vir_sym, occ_sym, integrals, amplitudes)])
    zero_out, tab, *spares = pl.pallas_call(
        functools.partial(plan_kernel, t),
        out_shape=(pltpu.HBM((occ_rows, cols), bf16), pltpu.SMEM((t.size,), i32))
        + tuple(
            pltpu.HBM((c, BLK, BLK), bf16) for c in chunks[1:] for _ in range(n_occ - 1)
        ),
        in_specs=[SMEM, SMEM, SMEM, ANY],
        out_specs=(HBM, SMEM) + (HBM,) * ((n_occ - 1) * (len(chunks) - 1)),
        scratch_shapes=[
            pltpu.VMEM((BLK, cols), bf16),
            pltpu.SemaphoreType.DMA((occ_rows // BLK,)),
        ],
        compiler_params=pltpu.CompilerParams(vmem_limit_bytes=4 * 2**20),
        name="plan",
    )(*[away(x) for x in (k_sym, vir_sym, occ_sym)], pay)

    shifts = tuple(range(1, n_occ))

    def across(x, shift):
        return lax.ppermute(x, "occ", [(i, (i + shift) % n_occ) for i in range(n_occ)])

    heads = [across(packed[0], shift) for shift in shifts]

    bits = [1 << b for b in range(n_vir.bit_length() - 1)][::-1]
    masks = [0]
    for bit in bits:
        masks = masks + [m ^ bit for m in masks]
    if width == BLK:
        parts = [pay]
        for bit in bits:
            pairs = [(i, i ^ bit) for i in range(n_vir)]
            parts = parts + [lax.ppermute(p, "vir", pairs) for p in parts]
            if len(parts) == 8:
                parts[5], zero_out = lax.optimization_barrier((parts[5], zero_out))
    else:
        whole = pay[None]
        for bit in bits:
            pairs = [(i, i ^ bit) for i in range(n_vir)]
            whole = jnp.concatenate([whole, lax.ppermute(whole, "vir", pairs)])
        place = [masks.index(m) for m in range(n_vir)]
        order = jnp.asarray(place, i32)[
            jnp.arange(n_vir, dtype=i32) ^ lax.axis_index("vir").astype(i32)
        ]
        whole = whole[order].transpose(1, 0, 2).reshape(rows, kblocks, BLK)
        parts, masks = [whole.transpose(1, 0, 2)], []

    amp, most = pl.pallas_call(
        functools.partial(sort_kernel, tuple(masks)),
        out_shape=(
            pltpu.VMEM((kblocks, MAXO * BLK, BLK), bf16),
            jax.ShapeDtypeStruct((1,), i32),
        ),
        in_specs=[VMEM] * len(parts),
        out_specs=(VMEM, SMEM),
        compiler_params=pltpu.CompilerParams(vmem_limit_bytes=8 * 2**20),
        name="sort",
    )(*parts)

    n = len(shifts)
    spares = [spares[c * n : (c + 1) * n] for c in range(len(chunks) - 1)]

    def more(level, place, operands):
        if level == len(chunks):
            return []
        return lax.cond(
            most[0] > place,
            lambda packed, spares: [[across(packed[0], shift) for shift in shifts]]
            + more(level + 1, place + chunks[level], (packed[1:], spares[1:])),
            lambda packed, spares: list(spares),
            *operands,
        )

    rests = more(1, first_cap, (packed[1:], spares))
    heads = [packed[0]] + heads
    rests = [x for own, others in zip(packed[1:], rests) for x in [own, *others]]
    return pl.pallas_call(
        functools.partial(finish_kernel, t, chunks),
        out_shape=jax.ShapeDtypeStruct((occ_rows, cols), bf16),
        in_specs=[SMEM] + [VMEM] * (1 + n_occ) + [ANY] * len(rests) + [HBM],
        out_specs=HBM,
        scratch_shapes=[
            pltpu.VMEM((MAXB, MAXO * BLK, BLK), f32),
            pltpu.VMEM((vblocks, MAXO * BLK, BLK), bf16),
            pltpu.VMEM((n_occ, cap, BLK, BLK), bf16),
            pltpu.SMEM((1,), i32),
            pltpu.SemaphoreType.DMA((vblocks * MAXO,)),
            pltpu.SemaphoreType.DMA((max(len(rests), 1),)),
        ],
        input_output_aliases={2 + n_occ + len(rests): 0},
        compiler_params=pltpu.CompilerParams(vmem_limit_bytes=24 * 2**20),
        name="finish",
    )(tab, *[here(x) for x in (amp, *heads)], *rests, zero_out)


def solution(mesh):
    return jax.shard_map(
        functools.partial(per_device, mesh.shape["occ"], mesh.shape["vir"]),
        mesh=mesh,
        in_specs=(P("occ", "vir"), P("occ", "vir"), P("occ"), P("vir"), P()),
        out_specs=P("occ", "vir"),
        check_vma=False,
    )
```

```python
import functools

import jax
import jax.numpy as jnp
from jax import lax
from jax.experimental import pallas as pl
from jax.experimental.pallas import tpu as pltpu
from jax.sharding import PartitionSpec as P

BLK = 128
IRREPS = 8
MAXO = 2
MAXB = 5
INFO = 16

SMEM = pl.BlockSpec(memory_space=pltpu.SMEM)
VMEM = pl.BlockSpec(memory_space=pltpu.VMEM)
ANY = pl.BlockSpec(memory_space=pl.ANY)
HBM = pl.BlockSpec(memory_space=pltpu.HBM)


def here(x):
    return pltpu.with_memory_space_constraint(x, pltpu.VMEM)


def away(x):
    return pltpu.with_memory_space_constraint(x, pltpu.HBM)


class Table:
    def __init__(self, n_occ, kblocks, vblocks):
        self.n_occ, self.own, self.vblocks = n_occ, kblocks // n_occ, vblocks
        self.nk = 0
        self.kbl = self.nk + n_occ * IRREPS
        self.cnt = self.kbl + n_occ * IRREPS * self.own
        self.vbl = self.cnt + IRREPS
        self.slot = self.vbl + IRREPS * MAXB
        self.off = self.slot + IRREPS * MAXO
        self.total = self.off + n_occ * vblocks
        self.active = self.total + n_occ
        self.size = self.active + 1 + IRREPS


def contraction_lists(t, ksym, tab, halves):
    for half in halves:
        for s in range(IRREPS):
            tab[t.nk + half * IRREPS + s] = 0
        for i in range(t.own):
            kb = half * t.own + i
            row = half * IRREPS + ksym[kb]
            rank = tab[t.nk + row]
            tab[t.kbl + row * t.own + rank] = kb
            tab[t.nk + row] = rank + 1


def pack_kernel(t, chunks, ksym, vsym, osym, v_ref, a_ref, *refs):
    packed, (pay, tab, sems, pay_sems) = refs[: len(chunks)], refs[len(chunks) :]
    own, vblocks, oblocks = t.own, t.vblocks, osym.shape[0]
    width = a_ref.shape[1]
    me = lax.axis_index("occ")
    others = tuple(lax.rem(me + d, t.n_occ) for d in range(1, t.n_occ))
    contraction_lists(t, ksym, tab, [me])

    def block(row, rank, vb):
        kb = tab[t.kbl + row * own + rank] - me * own
        return v_ref.at[
            pl.ds(pl.multiple_of(kb * BLK, BLK), BLK),
            pl.ds(pl.multiple_of(vb * BLK, BLK), BLK),
        ]

    total = jnp.int32(0)
    for vb in range(vblocks):
        row = me * IRREPS + vsym[vb]
        n = tab[t.nk + row]

        @pl.loop(0, n)
        def _(rank, vb=vb, row=row, place0=total):
            place = place0 + rank

            def start(chunk, place0):
                pltpu.make_async_copy(
                    block(row, rank, vb), chunk.at[place - place0], sems.at[place]
                ).start()

            @pl.when(place < chunks[0])
            def _():
                start(packed[0], 0)

            @pl.when(place >= chunks[0])
            def _():
                place0 = chunks[0]
                for size, chunk in zip(chunks[1:], packed[1:]):

                    @pl.when((place >= place0) & (place < place0 + size))
                    def _(chunk=chunk, place0=place0):
                        start(chunk, place0)

                    place0 += size

        total = total + n

    vir = lax.axis_index("vir")
    step = min(width, BLK)
    copies = []
    for q in range(width // step):
        s = ksym[(vir * width + q * step) // BLK]
        cols = slice(q * step, (q + 1) * step)
        found = jnp.int32(0)
        slots = [jnp.int32(-1)] * MAXO
        for ob in range(oblocks):
            match = osym[ob] == s
            slots = [
                jnp.where(match & (found == i), ob, slot) for i, slot in enumerate(slots)
            ]
            found = found + match.astype(jnp.int32)
        for i, ob in enumerate(slots):
            copy = pltpu.make_async_copy(
                a_ref.at[
                    pl.ds(pl.multiple_of(jnp.maximum(ob, 0) * BLK, BLK), BLK),
                    pl.ds(q * step, step),
                ],
                pay.at[pl.ds(i * BLK, BLK), pl.ds(q * step, step)],
                pay_sems.at[q * MAXO + i],
            )
            copies.append((ob, copy))

            @pl.when(ob >= 0)
            def _(copy=copy):
                copy.start()

            @pl.when(ob < 0)
            def _(i=i, cols=cols):
                pay[i * BLK : (i + 1) * BLK, cols] = jnp.zeros((BLK, step), jnp.bfloat16)

    contraction_lists(t, ksym, tab, others)
    most = total
    for half in others:
        other = jnp.int32(0)
        for vb in range(vblocks):
            other = other + tab[t.nk + half * IRREPS + vsym[vb]]
        most = jnp.maximum(most, other)

    pay[MAXO * BLK :, :] = jnp.full(
        (INFO, width), most.astype(jnp.float32), jnp.float32
    ).astype(jnp.bfloat16)

    for ob, copy in copies:

        @pl.when(ob >= 0)
        def _(copy=copy):
            copy.wait()

    @pl.loop(0, total)
    def _(place):
        pltpu.make_async_copy(
            v_ref.at[pl.ds(0, BLK), pl.ds(0, BLK)], packed[0].at[0], sems.at[place]
        ).wait()


def plan_kernel(t, ksym, vsym, osym, after, out, tab, *refs):
    del after
    zeros, sems = refs[-2:]
    zeros[...] = jnp.zeros_like(zeros)
    fills = [
        pltpu.make_async_copy(zeros, out.at[pl.ds(i * BLK, BLK)], sems.at[i])
        for i in range(out.shape[0] // BLK)
    ]
    for fill in fills:
        fill.start()

    contraction_lists(t, ksym, tab, range(t.n_occ))
    for s in range(IRREPS):
        tab[t.cnt + s] = 0
        for slot in range(MAXO):
            tab[t.slot + s * MAXO + slot] = -1
    for ob in range(osym.shape[0]):
        s = osym[ob]
        used = (tab[t.slot + s * MAXO] >= 0).astype(jnp.int32)
        tab[t.slot + s * MAXO + used] = ob

    def count(vb, places):
        s = vsym[vb]
        rank = tab[t.cnt + s]
        tab[t.vbl + s * MAXB + rank] = vb
        tab[t.cnt + s] = rank + 1
        new = []
        for half, place in enumerate(places):
            tab[t.off + half * t.vblocks + vb] = place
            new.append(place + tab[t.nk + half * IRREPS + s])
        return tuple(new)

    totals = lax.fori_loop(0, t.vblocks, count, (jnp.int32(0),) * t.n_occ)
    for half, total in enumerate(totals):
        tab[t.total + half] = total
    tab[t.active] = 0
    for s in range(IRREPS):

        @pl.when((tab[t.cnt + s] > 0) & (tab[t.slot + s * MAXO] >= 0))
        def _(s=s):
            used = tab[t.active]
            tab[t.active + 1 + used] = s
            tab[t.active] = used + 1
    for fill in fills:
        fill.wait()


def each_irrep(t, tab, act, variants):
    @pl.loop(0, tab[t.active])
    def _(i):
        s = tab[t.active + 1 + i]
        count = tab[t.cnt + s]
        rows = jnp.int32(BLK)
        for slot in range(1, MAXO):
            more = tab[t.slot + s * MAXO + slot] >= 0
            rows = jnp.where(more, (slot + 1) * BLK, rows)
        todo = count > 0
        for have, width in variants:
            fits = todo & (rows <= have) & (count <= width)

            @pl.when(fits)
            def _():
                act(
                    s,
                    have,
                    [
                        jnp.where(j < count, tab[t.vbl + s * MAXB + j], -1)
                        for j in range(width)
                    ],
                )

            todo = todo & jnp.logical_not(fits)


def multiply(t, tab, halves, s, rows, vbs, amp, sources, acc):
    bases = [half * IRREPS + s for half in halves]
    counts = [tab[t.nk + row] for row in bases]
    offs = [
        [jnp.where(vb >= 0, tab[t.off + half * t.vblocks + jnp.maximum(vb, 0)], 0) for vb in vbs]
        for half in halves
    ]
    steps = counts[0]
    for count in counts[1:]:
        steps = jnp.maximum(steps, count)

    def terms(rank):
        lefts, rights = [], [[] for _ in vbs]
        for row, count, places, source in zip(bases, counts, offs, sources):
            there = rank < count
            here = jnp.where(there, rank, 0)
            kb = jnp.where(there, tab[t.kbl + row * t.own + here], 0)
            left = amp[kb, :rows, :]
            lefts.append(jnp.where(there, left, jnp.zeros_like(left)))
            for place, column in zip(places, rights):
                right = source[jnp.where(there, place + here, 0)]
                column.append(jnp.where(there, right, jnp.zeros_like(right)))
        left = jnp.concatenate(lefts, axis=1)
        return [
            jnp.dot(
                left,
                jnp.concatenate(column, axis=0),
                preferred_element_type=jnp.float32,
            )
            for column in rights
        ]

    for j, part in enumerate(terms(jnp.int32(0))):
        acc[j, :rows, :] = part

    @pl.loop(1, steps)
    def _(rank):
        for j, part in enumerate(terms(rank)):
            acc[j, :rows, :] += part


def sort_kernel(masks, *refs):
    parts, (amp, most) = refs[:-2], refs[-2:]
    peak = parts[0][..., MAXO * BLK :, :].astype(jnp.float32)
    if masks:
        me = lax.axis_index("vir")
        for mask, part in zip(masks, parts):
            amp[me ^ mask] = part[: MAXO * BLK, :]
            peak = jnp.maximum(peak, part[MAXO * BLK :, :].astype(jnp.float32))
    else:
        amp[...] = parts[0][:, : MAXO * BLK, :]
    most[0] = jnp.max(peak).astype(jnp.int32)


def finish_kernel(t, chunks, tab, amp, *refs):
    n = t.n_occ
    heads, rests = refs[:n], refs[n : n * len(chunks)]
    _, out, acc, stage, blocks, sent, sems, load_sems = refs[n * len(chunks) :]
    me = lax.axis_index("occ")
    halves = [lax.rem(me - shift + n, n) for shift in range(n)]

    sent[0] = 0

    def send(s, slot, vb, index):
        ob = tab[t.slot + s * MAXO + slot]
        return pltpu.make_async_copy(
            stage.at[vb, pl.ds(slot * BLK, BLK)],
            out.at[
                pl.ds(pl.multiple_of(ob * BLK, BLK), BLK),
                pl.ds(pl.multiple_of(vb * BLK, BLK), BLK),
            ],
            sems.at[index],
        )

    def store(s, slot, j, vb):
        rows = slice(slot * BLK, (slot + 1) * BLK)
        stage[vb, rows, :] = acc[j, rows, :].astype(jnp.bfloat16)
        index = sent[0]
        send(s, slot, vb, index).start()
        sent[0] = index + 1

    def products(sources, variants):
        def act(s, rows, vbs):
            multiply(t, tab, halves, s, rows, vbs, amp, sources, acc)
            for j, vb in enumerate(vbs):
                for slot in range(rows // BLK):

                    @pl.when((vb >= 0) & (tab[t.slot + s * MAXO + slot] >= 0))
                    def _():
                        store(s, slot, j, vb)

        each_irrep(t, tab, act, variants)

    whole = ((MAXO * BLK, MAXB),)
    usual = ((BLK, 2), (BLK, 3), (BLK, MAXB), (MAXO * BLK, 3)) + whole

    most = tab[t.total]
    for half in range(1, n):
        most = jnp.maximum(most, tab[t.total + half])

    @pl.when(most <= chunks[0])
    def _():
        products(heads, usual)

    @pl.when(most > chunks[0])
    def _():
        def load(act):
            place = chunks[0]
            for c, size in enumerate(chunks[1:]):

                @pl.when(most > place)
                def _(c=c, size=size, place=place):
                    for i in range(n):
                        act(
                            pltpu.make_async_copy(
                                rests[c * n + i],
                                blocks.at[i, pl.ds(place, size)],
                                load_sems.at[c * n + i],
                            )
                        )

                place += size

        load(lambda copy: copy.start())
        for i in range(n):
            blocks[i, : chunks[0]] = heads[i][...]
        load(lambda copy: copy.wait())
        products([blocks.at[i] for i in range(n)], usual)

    @pl.loop(0, sent[0])
    def _(index):
        pltpu.make_async_copy(
            stage.at[0, pl.ds(0, BLK)],
            out.at[pl.ds(0, BLK), pl.ds(0, BLK)],
            sems.at[index],
        ).wait()


def per_device(n_occ, n_vir, amplitudes, integrals, occ_sym, vir_sym, k_sym):
    occ_rows, width = amplitudes.shape
    kblocks = k_sym.shape[0]
    vblocks = vir_sym.shape[0]
    cols = vblocks * BLK
    t = Table(n_occ, kblocks, vblocks)
    cap = t.own * MAXB
    first_cap = (cap * 27 + 39) // 40
    more_cap = (cap - first_cap) // 3
    chunks = tuple(c for c in (first_cap, more_cap, cap - first_cap - more_cap) if c)
    rows = MAXO * BLK + INFO
    bf16, f32, i32 = jnp.bfloat16, jnp.float32, jnp.int32

    *packed, pay = pl.pallas_call(
        functools.partial(pack_kernel, t, chunks),
        out_shape=tuple(pltpu.VMEM((c, BLK, BLK), bf16) for c in chunks)
        + (pltpu.VMEM((rows, width), bf16),),
        in_specs=[SMEM, SMEM, SMEM, HBM, HBM],
        out_specs=(VMEM,) * (len(chunks) + 1),
        scratch_shapes=[
            pltpu.SMEM((t.size,), i32),
            pltpu.SemaphoreType.DMA((cap,)),
            pltpu.SemaphoreType.DMA((MAXO * max(width // BLK, 1),)),
        ],
        compiler_params=pltpu.CompilerParams(vmem_limit_bytes=8 * 2**20),
        name="pack",
    )(*[away(x) for x in (k_sym, vir_sym, occ_sym, integrals, amplitudes)])
    zero_out, tab, *spares = pl.pallas_call(
        functools.partial(plan_kernel, t),
        out_shape=(pltpu.HBM((occ_rows, cols), bf16), pltpu.SMEM((t.size,), i32))
        + tuple(
            pltpu.HBM((c, BLK, BLK), bf16) for c in chunks[1:] for _ in range(n_occ - 1)
        ),
        in_specs=[SMEM, SMEM, SMEM, ANY],
        out_specs=(HBM, SMEM) + (HBM,) * ((n_occ - 1) * (len(chunks) - 1)),
        scratch_shapes=[
            pltpu.VMEM((BLK, cols), bf16),
            pltpu.SemaphoreType.DMA((occ_rows // BLK,)),
        ],
        compiler_params=pltpu.CompilerParams(vmem_limit_bytes=4 * 2**20),
        name="plan",
    )(*[away(x) for x in (k_sym, vir_sym, occ_sym)], pay)

    shifts = tuple(range(1, n_occ))

    def across(x, shift):
        return lax.ppermute(x, "occ", [(i, (i + shift) % n_occ) for i in range(n_occ)])

    heads = [across(packed[0], shift) for shift in shifts]

    bits = [1 << b for b in range(n_vir.bit_length() - 1)][::-1]
    masks = [0]
    for bit in bits:
        masks = masks + [m ^ bit for m in masks]
    if width == BLK:
        parts = [pay]
        for bit in bits:
            pairs = [(i, i ^ bit) for i in range(n_vir)]
            parts = parts + [lax.ppermute(p, "vir", pairs) for p in parts]
            if len(parts) == 8:
                parts[5], zero_out = lax.optimization_barrier((parts[5], zero_out))
    else:
        whole = pay[None]
        for bit in bits:
            pairs = [(i, i ^ bit) for i in range(n_vir)]
            whole = jnp.concatenate([whole, lax.ppermute(whole, "vir", pairs)])
        place = [masks.index(m) for m in range(n_vir)]
        order = jnp.asarray(place, i32)[
            jnp.arange(n_vir, dtype=i32) ^ lax.axis_index("vir").astype(i32)
        ]
        whole = whole[order].transpose(1, 0, 2).reshape(rows, kblocks, BLK)
        parts, masks = [whole.transpose(1, 0, 2)], []

    amp, most = pl.pallas_call(
        functools.partial(sort_kernel, tuple(masks)),
        out_shape=(
            pltpu.VMEM((kblocks, MAXO * BLK, BLK), bf16),
            jax.ShapeDtypeStruct((1,), i32),
        ),
        in_specs=[VMEM] * len(parts),
        out_specs=(VMEM, SMEM),
        compiler_params=pltpu.CompilerParams(vmem_limit_bytes=8 * 2**20),
        name="sort",
    )(*parts)

    n = len(shifts)
    spares = [spares[c * n : (c + 1) * n] for c in range(len(chunks) - 1)]

    def more(level, place, operands):
        if level == len(chunks):
            return []
        return lax.cond(
            most[0] > place,
            lambda packed, spares: [[across(packed[0], shift) for shift in shifts]]
            + more(level + 1, place + chunks[level], (packed[1:], spares[1:])),
            lambda packed, spares: list(spares),
            *operands,
        )

    rests = more(1, first_cap, (packed[1:], spares))
    heads = [packed[0]] + heads
    rests = [x for own, others in zip(packed[1:], rests) for x in [own, *others]]
    return pl.pallas_call(
        functools.partial(finish_kernel, t, chunks),
        out_shape=jax.ShapeDtypeStruct((occ_rows, cols), bf16),
        in_specs=[SMEM] + [VMEM] * (1 + n_occ) + [ANY] * len(rests) + [HBM],
        out_specs=HBM,
        scratch_shapes=[
            pltpu.VMEM((MAXB, MAXO * BLK, BLK), f32),
            pltpu.VMEM((vblocks, MAXO * BLK, BLK), bf16),
            pltpu.VMEM((n_occ, cap, BLK, BLK), bf16),
            pltpu.SMEM((1,), i32),
            pltpu.SemaphoreType.DMA((vblocks * MAXO,)),
            pltpu.SemaphoreType.DMA((max(len(rests), 1),)),
        ],
        input_output_aliases={2 + n_occ + len(rests): 0},
        compiler_params=pltpu.CompilerParams(vmem_limit_bytes=24 * 2**20),
        name="finish",
    )(tab, *[here(x) for x in (amp, *heads)], *rests, zero_out)


def solution(mesh):
    return jax.shard_map(
        functools.partial(per_device, mesh.shape["occ"], mesh.shape["vir"]),
        mesh=mesh,
        in_specs=(P("occ", "vir"), P("occ", "vir"), P("occ"), P("vir"), P()),
        out_specs=P("occ", "vir"),
        check_vma=False,
    )
```

```python
import functools

import jax
import jax.numpy as jnp
from jax import lax
from jax.experimental import pallas as pl
from jax.experimental.pallas import tpu as pltpu
from jax.sharding import PartitionSpec as P

BLK = 128
IRREPS = 8
MAXO = 2
MAXB = 5
INFO = 16

SMEM = pl.BlockSpec(memory_space=pltpu.SMEM)
VMEM = pl.BlockSpec(memory_space=pltpu.VMEM)
ANY = pl.BlockSpec(memory_space=pl.ANY)
HBM = pl.BlockSpec(memory_space=pltpu.HBM)


def here(x):
    return pltpu.with_memory_space_constraint(x, pltpu.VMEM)


def away(x):
    return pltpu.with_memory_space_constraint(x, pltpu.HBM)


class Table:
    def __init__(self, n_occ, kblocks, vblocks):
        self.n_occ, self.own, self.vblocks = n_occ, kblocks // n_occ, vblocks
        self.nk = 0
        self.kbl = self.nk + n_occ * IRREPS
        self.cnt = self.kbl + n_occ * IRREPS * self.own
        self.vbl = self.cnt + IRREPS
        self.slot = self.vbl + IRREPS * MAXB
        self.off = self.slot + IRREPS * MAXO
        self.total = self.off + n_occ * vblocks
        self.active = self.total + n_occ
        self.size = self.active + 1 + IRREPS


def contraction_lists(t, ksym, tab, halves):
    for half in halves:
        for s in range(IRREPS):
            tab[t.nk + half * IRREPS + s] = 0
        for i in range(t.own):
            kb = half * t.own + i
            row = half * IRREPS + ksym[kb]
            rank = tab[t.nk + row]
            tab[t.kbl + row * t.own + rank] = kb
            tab[t.nk + row] = rank + 1


def pack_kernel(t, chunks, ksym, vsym, osym, v_ref, a_ref, *refs):
    packed, (pay, tab, sems, pay_sems) = refs[: len(chunks)], refs[len(chunks) :]
    own, vblocks, oblocks = t.own, t.vblocks, osym.shape[0]
    width = a_ref.shape[1]
    me = lax.axis_index("occ")
    others = tuple(lax.rem(me + d, t.n_occ) for d in range(1, t.n_occ))
    contraction_lists(t, ksym, tab, [me])

    def block(row, rank, vb):
        kb = tab[t.kbl + row * own + rank] - me * own
        return v_ref.at[
            pl.ds(pl.multiple_of(kb * BLK, BLK), BLK),
            pl.ds(pl.multiple_of(vb * BLK, BLK), BLK),
        ]

    total = jnp.int32(0)
    for vb in range(vblocks):
        row = me * IRREPS + vsym[vb]
        n = tab[t.nk + row]

        @pl.loop(0, n)
        def _(rank, vb=vb, row=row, place0=total):
            place = place0 + rank

            def start(chunk, place0):
                pltpu.make_async_copy(
                    block(row, rank, vb), chunk.at[place - place0], sems.at[place]
                ).start()

            @pl.when(place < chunks[0])
            def _():
                start(packed[0], 0)

            @pl.when(place >= chunks[0])
            def _():
                place0 = chunks[0]
                for size, chunk in zip(chunks[1:], packed[1:]):

                    @pl.when((place >= place0) & (place < place0 + size))
                    def _(chunk=chunk, place0=place0):
                        start(chunk, place0)

                    place0 += size

        total = total + n

    vir = lax.axis_index("vir")
    step = min(width, BLK)
    copies = []
    for q in range(width // step):
        s = ksym[(vir * width + q * step) // BLK]
        cols = slice(q * step, (q + 1) * step)
        found = jnp.int32(0)
        slots = [jnp.int32(-1)] * MAXO
        for ob in range(oblocks):
            match = osym[ob] == s
            slots = [
                jnp.where(match & (found == i), ob, slot) for i, slot in enumerate(slots)
            ]
            found = found + match.astype(jnp.int32)
        for i, ob in enumerate(slots):
            copy = pltpu.make_async_copy(
                a_ref.at[
                    pl.ds(pl.multiple_of(jnp.maximum(ob, 0) * BLK, BLK), BLK),
                    pl.ds(q * step, step),
                ],
                pay.at[pl.ds(i * BLK, BLK), pl.ds(q * step, step)],
                pay_sems.at[q * MAXO + i],
            )
            copies.append((ob, copy))

            @pl.when(ob >= 0)
            def _(copy=copy):
                copy.start()

            @pl.when(ob < 0)
            def _(i=i, cols=cols):
                pay[i * BLK : (i + 1) * BLK, cols] = jnp.zeros((BLK, step), jnp.bfloat16)

    contraction_lists(t, ksym, tab, others)
    most = total
    for half in others:
        other = jnp.int32(0)
        for vb in range(vblocks):
            other = other + tab[t.nk + half * IRREPS + vsym[vb]]
        most = jnp.maximum(most, other)

    pay[MAXO * BLK :, :] = jnp.full(
        (INFO, width), most.astype(jnp.float32), jnp.float32
    ).astype(jnp.bfloat16)

    for ob, copy in copies:

        @pl.when(ob >= 0)
        def _(copy=copy):
            copy.wait()

    @pl.loop(0, total)
    def _(place):
        pltpu.make_async_copy(
            v_ref.at[pl.ds(0, BLK), pl.ds(0, BLK)], packed[0].at[0], sems.at[place]
        ).wait()


def plan_kernel(t, ksym, vsym, osym, after, out, tab, *refs):
    del after
    zeros, sems = refs[-2:]
    zeros[...] = jnp.zeros_like(zeros)
    fills = [
        pltpu.make_async_copy(zeros, out.at[pl.ds(i * BLK, BLK)], sems.at[i])
        for i in range(out.shape[0] // BLK)
    ]
    for fill in fills:
        fill.start()

    contraction_lists(t, ksym, tab, range(t.n_occ))
    for s in range(IRREPS):
        tab[t.cnt + s] = 0
        for slot in range(MAXO):
            tab[t.slot + s * MAXO + slot] = -1
    for ob in range(osym.shape[0]):
        s = osym[ob]
        used = (tab[t.slot + s * MAXO] >= 0).astype(jnp.int32)
        tab[t.slot + s * MAXO + used] = ob

    def count(vb, places):
        s = vsym[vb]
        rank = tab[t.cnt + s]
        tab[t.vbl + s * MAXB + rank] = vb
        tab[t.cnt + s] = rank + 1
        new = []
        for half, place in enumerate(places):
            tab[t.off + half * t.vblocks + vb] = place
            new.append(place + tab[t.nk + half * IRREPS + s])
        return tuple(new)

    totals = lax.fori_loop(0, t.vblocks, count, (jnp.int32(0),) * t.n_occ)
    for half, total in enumerate(totals):
        tab[t.total + half] = total
    tab[t.active] = 0
    for slots in range(MAXO, 0, -1):
        for s in range(IRREPS):
            fit = tab[t.slot + s * MAXO + slots - 1] >= 0
            if slots < MAXO:
                fit = fit & (tab[t.slot + s * MAXO + slots] < 0)

            @pl.when((tab[t.cnt + s] > 0) & fit)
            def _(s=s):
                used = tab[t.active]
                tab[t.active + 1 + used] = s
                tab[t.active] = used + 1
    for fill in fills:
        fill.wait()


def each_irrep(t, tab, act, variants):
    @pl.loop(0, tab[t.active])
    def _(i):
        s = tab[t.active + 1 + i]
        count = tab[t.cnt + s]
        rows = jnp.int32(BLK)
        for slot in range(1, MAXO):
            more = tab[t.slot + s * MAXO + slot] >= 0
            rows = jnp.where(more, (slot + 1) * BLK, rows)
        todo = count > 0
        for have, width in variants:
            fits = todo & (rows <= have) & (count <= width)

            @pl.when(fits)
            def _():
                act(
                    s,
                    have,
                    [
                        jnp.where(j < count, tab[t.vbl + s * MAXB + j], -1)
                        for j in range(width)
                    ],
                )

            todo = todo & jnp.logical_not(fits)


def multiply(t, tab, halves, s, rows, vbs, amp, sources, acc):
    bases = [half * IRREPS + s for half in halves]
    counts = [tab[t.nk + row] for row in bases]
    offs = [
        [jnp.where(vb >= 0, tab[t.off + half * t.vblocks + jnp.maximum(vb, 0)], 0) for vb in vbs]
        for half in halves
    ]
    steps = counts[0]
    for count in counts[1:]:
        steps = jnp.maximum(steps, count)

    def terms(rank):
        lefts, rights = [], [[] for _ in vbs]
        for row, count, places, source in zip(bases, counts, offs, sources):
            there = rank < count
            here = jnp.where(there, rank, 0)
            kb = jnp.where(there, tab[t.kbl + row * t.own + here], 0)
            left = amp[kb, :rows, :]
            lefts.append(jnp.where(there, left, jnp.zeros_like(left)))
            for place, column in zip(places, rights):
                right = source[jnp.where(there, place + here, 0)]
                column.append(jnp.where(there, right, jnp.zeros_like(right)))
        left = jnp.concatenate(lefts, axis=1)
        return [
            jnp.dot(
                left,
                jnp.concatenate(column, axis=0),
                preferred_element_type=jnp.float32,
            )
            for column in rights
        ]

    for j, part in enumerate(terms(jnp.int32(0))):
        acc[j, :rows, :] = part

    @pl.loop(1, steps)
    def _(rank):
        for j, part in enumerate(terms(rank)):
            acc[j, :rows, :] += part


def sort_kernel(masks, *refs):
    parts, (amp, most) = refs[:-2], refs[-2:]
    peak = parts[0][..., MAXO * BLK :, :].astype(jnp.float32)
    if masks:
        me = lax.axis_index("vir")
        for mask, part in zip(masks, parts):
            amp[me ^ mask] = part[: MAXO * BLK, :]
            peak = jnp.maximum(peak, part[MAXO * BLK :, :].astype(jnp.float32))
    else:
        amp[...] = parts[0][:, : MAXO * BLK, :]
    most[0] = jnp.max(peak).astype(jnp.int32)


def finish_kernel(t, chunks, tab, amp, *refs):
    n = t.n_occ
    heads, rests = refs[:n], refs[n : n * len(chunks)]
    _, out, acc, stage, blocks, sent, sems, load_sems = refs[n * len(chunks) :]
    me = lax.axis_index("occ")
    halves = [lax.rem(me - shift + n, n) for shift in range(n)]

    sent[0] = 0

    def send(s, slot, vb, index):
        ob = tab[t.slot + s * MAXO + slot]
        return pltpu.make_async_copy(
            stage.at[vb, pl.ds(slot * BLK, BLK)],
            out.at[
                pl.ds(pl.multiple_of(ob * BLK, BLK), BLK),
                pl.ds(pl.multiple_of(vb * BLK, BLK), BLK),
            ],
            sems.at[index],
        )

    def store(s, slot, j, vb):
        rows = slice(slot * BLK, (slot + 1) * BLK)
        stage[vb, rows, :] = acc[j, rows, :].astype(jnp.bfloat16)
        index = sent[0]
        send(s, slot, vb, index).start()
        sent[0] = index + 1

    def products(sources, variants):
        def act(s, rows, vbs):
            multiply(t, tab, halves, s, rows, vbs, amp, sources, acc)
            for j, vb in enumerate(vbs):
                for slot in range(rows // BLK):

                    @pl.when((vb >= 0) & (tab[t.slot + s * MAXO + slot] >= 0))
                    def _():
                        store(s, slot, j, vb)

        each_irrep(t, tab, act, variants)

    whole = ((MAXO * BLK, MAXB),)
    usual = ((BLK, 2), (BLK, 3), (BLK, MAXB), (MAXO * BLK, 3)) + whole

    most = tab[t.total]
    for half in range(1, n):
        most = jnp.maximum(most, tab[t.total + half])

    @pl.when(most <= chunks[0])
    def _():
        products(heads, usual)

    @pl.when(most > chunks[0])
    def _():
        def load(act):
            place = chunks[0]
            for c, size in enumerate(chunks[1:]):

                @pl.when(most > place)
                def _(c=c, size=size, place=place):
                    for i in range(n):
                        act(
                            pltpu.make_async_copy(
                                rests[c * n + i],
                                blocks.at[i, pl.ds(place, size)],
                                load_sems.at[c * n + i],
                            )
                        )

                place += size

        load(lambda copy: copy.start())
        for i in range(n):
            blocks[i, : chunks[0]] = heads[i][...]
        load(lambda copy: copy.wait())
        products([blocks.at[i] for i in range(n)], usual)

    @pl.loop(0, sent[0])
    def _(index):
        pltpu.make_async_copy(
            stage.at[0, pl.ds(0, BLK)],
            out.at[pl.ds(0, BLK), pl.ds(0, BLK)],
            sems.at[index],
        ).wait()


def per_device(n_occ, n_vir, amplitudes, integrals, occ_sym, vir_sym, k_sym):
    occ_rows, width = amplitudes.shape
    kblocks = k_sym.shape[0]
    vblocks = vir_sym.shape[0]
    cols = vblocks * BLK
    t = Table(n_occ, kblocks, vblocks)
    cap = t.own * MAXB
    first_cap = (cap * 27 + 39) // 40
    more_cap = (cap - first_cap) // 3
    chunks = tuple(c for c in (first_cap, more_cap, cap - first_cap - more_cap) if c)
    rows = MAXO * BLK + INFO
    bf16, f32, i32 = jnp.bfloat16, jnp.float32, jnp.int32

    *packed, pay = pl.pallas_call(
        functools.partial(pack_kernel, t, chunks),
        out_shape=tuple(pltpu.VMEM((c, BLK, BLK), bf16) for c in chunks)
        + (pltpu.VMEM((rows, width), bf16),),
        in_specs=[SMEM, SMEM, SMEM, HBM, HBM],
        out_specs=(VMEM,) * (len(chunks) + 1),
        scratch_shapes=[
            pltpu.SMEM((t.size,), i32),
            pltpu.SemaphoreType.DMA((cap,)),
            pltpu.SemaphoreType.DMA((MAXO * max(width // BLK, 1),)),
        ],
        compiler_params=pltpu.CompilerParams(vmem_limit_bytes=8 * 2**20),
        name="pack",
    )(*[away(x) for x in (k_sym, vir_sym, occ_sym, integrals, amplitudes)])
    zero_out, tab, *spares = pl.pallas_call(
        functools.partial(plan_kernel, t),
        out_shape=(pltpu.HBM((occ_rows, cols), bf16), pltpu.SMEM((t.size,), i32))
        + tuple(
            pltpu.HBM((c, BLK, BLK), bf16) for c in chunks[1:] for _ in range(n_occ - 1)
        ),
        in_specs=[SMEM, SMEM, SMEM, ANY],
        out_specs=(HBM, SMEM) + (HBM,) * ((n_occ - 1) * (len(chunks) - 1)),
        scratch_shapes=[
            pltpu.VMEM((BLK, cols), bf16),
            pltpu.SemaphoreType.DMA((occ_rows // BLK,)),
        ],
        compiler_params=pltpu.CompilerParams(vmem_limit_bytes=4 * 2**20),
        name="plan",
    )(*[away(x) for x in (k_sym, vir_sym, occ_sym)], pay)

    shifts = tuple(range(1, n_occ))

    def across(x, shift):
        return lax.ppermute(x, "occ", [(i, (i + shift) % n_occ) for i in range(n_occ)])

    heads = [across(packed[0], shift) for shift in shifts]

    bits = [1 << b for b in range(n_vir.bit_length() - 1)][::-1]
    masks = [0]
    for bit in bits:
        masks = masks + [m ^ bit for m in masks]
    if width == BLK:
        parts = [pay]
        for bit in bits:
            pairs = [(i, i ^ bit) for i in range(n_vir)]
            parts = parts + [lax.ppermute(p, "vir", pairs) for p in parts]
            if len(parts) == 8:
                parts[5], zero_out = lax.optimization_barrier((parts[5], zero_out))
    else:
        whole = pay[None]
        for bit in bits:
            pairs = [(i, i ^ bit) for i in range(n_vir)]
            whole = jnp.concatenate([whole, lax.ppermute(whole, "vir", pairs)])
        place = [masks.index(m) for m in range(n_vir)]
        order = jnp.asarray(place, i32)[
            jnp.arange(n_vir, dtype=i32) ^ lax.axis_index("vir").astype(i32)
        ]
        whole = whole[order].transpose(1, 0, 2).reshape(rows, kblocks, BLK)
        parts, masks = [whole.transpose(1, 0, 2)], []

    amp, most = pl.pallas_call(
        functools.partial(sort_kernel, tuple(masks)),
        out_shape=(
            pltpu.VMEM((kblocks, MAXO * BLK, BLK), bf16),
            jax.ShapeDtypeStruct((1,), i32),
        ),
        in_specs=[VMEM] * len(parts),
        out_specs=(VMEM, SMEM),
        compiler_params=pltpu.CompilerParams(vmem_limit_bytes=8 * 2**20),
        name="sort",
    )(*parts)

    n = len(shifts)
    spares = [spares[c * n : (c + 1) * n] for c in range(len(chunks) - 1)]

    def more(level, place, operands):
        if level == len(chunks):
            return []
        return lax.cond(
            most[0] > place,
            lambda packed, spares: [[across(packed[0], shift) for shift in shifts]]
            + more(level + 1, place + chunks[level], (packed[1:], spares[1:])),
            lambda packed, spares: list(spares),
            *operands,
        )

    rests = more(1, first_cap, (packed[1:], spares))
    heads = [packed[0]] + heads
    rests = [x for own, others in zip(packed[1:], rests) for x in [own, *others]]
    return pl.pallas_call(
        functools.partial(finish_kernel, t, chunks),
        out_shape=jax.ShapeDtypeStruct((occ_rows, cols), bf16),
        in_specs=[SMEM] + [VMEM] * (1 + n_occ) + [ANY] * len(rests) + [HBM],
        out_specs=HBM,
        scratch_shapes=[
            pltpu.VMEM((MAXB, MAXO * BLK, BLK), f32),
            pltpu.VMEM((vblocks, MAXO * BLK, BLK), bf16),
            pltpu.VMEM((n_occ, cap, BLK, BLK), bf16),
            pltpu.SMEM((1,), i32),
            pltpu.SemaphoreType.DMA((vblocks * MAXO,)),
            pltpu.SemaphoreType.DMA((max(len(rests), 1),)),
        ],
        input_output_aliases={2 + n_occ + len(rests): 0},
        compiler_params=pltpu.CompilerParams(vmem_limit_bytes=24 * 2**20),
        name="finish",
    )(tab, *[here(x) for x in (amp, *heads)], *rests, zero_out)


def solution(mesh):
    return jax.shard_map(
        functools.partial(per_device, mesh.shape["occ"], mesh.shape["vir"]),
        mesh=mesh,
        in_specs=(P("occ", "vir"), P("occ", "vir"), P("occ"), P("vir"), P()),
        out_specs=P("occ", "vir"),
        check_vma=False,
    )
```

```python
import functools

import jax
import jax.numpy as jnp
from jax import lax
from jax.experimental import pallas as pl
from jax.experimental.pallas import tpu as pltpu
from jax.sharding import PartitionSpec as P

BLK = 128
IRREPS = 8
MAXO = 2
MAXB = 5
INFO = 16

SMEM = pl.BlockSpec(memory_space=pltpu.SMEM)
VMEM = pl.BlockSpec(memory_space=pltpu.VMEM)
ANY = pl.BlockSpec(memory_space=pl.ANY)
HBM = pl.BlockSpec(memory_space=pltpu.HBM)


def here(x):
    return pltpu.with_memory_space_constraint(x, pltpu.VMEM)


def away(x):
    return pltpu.with_memory_space_constraint(x, pltpu.HBM)


class Table:
    def __init__(self, n_occ, kblocks, vblocks):
        self.n_occ, self.own, self.vblocks = n_occ, kblocks // n_occ, vblocks
        self.nk = 0
        self.kbl = self.nk + n_occ * IRREPS
        self.cnt = self.kbl + n_occ * IRREPS * self.own
        self.vbl = self.cnt + IRREPS
        self.slot = self.vbl + IRREPS * MAXB
        self.off = self.slot + IRREPS * MAXO
        self.total = self.off + n_occ * vblocks
        self.active = self.total + n_occ
        self.size = self.active + 1 + IRREPS


def contraction_lists(t, ksym, tab, halves):
    for half in halves:
        for s in range(IRREPS):
            tab[t.nk + half * IRREPS + s] = 0
        for i in range(t.own):
            kb = half * t.own + i
            row = half * IRREPS + ksym[kb]
            rank = tab[t.nk + row]
            tab[t.kbl + row * t.own + rank] = kb
            tab[t.nk + row] = rank + 1


def pack_kernel(t, chunks, ksym, vsym, osym, v_ref, a_ref, *refs):
    packed, (pay, tab, sems, pay_sems) = refs[: len(chunks)], refs[len(chunks) :]
    own, vblocks, oblocks = t.own, t.vblocks, osym.shape[0]
    width = a_ref.shape[1]
    me = lax.axis_index("occ")
    others = tuple(lax.rem(me + d, t.n_occ) for d in range(1, t.n_occ))
    contraction_lists(t, ksym, tab, [me])

    def block(row, rank, vb):
        kb = tab[t.kbl + row * own + rank] - me * own
        return v_ref.at[
            pl.ds(pl.multiple_of(kb * BLK, BLK), BLK),
            pl.ds(pl.multiple_of(vb * BLK, BLK), BLK),
        ]

    total = jnp.int32(0)
    for vb in range(vblocks):
        row = me * IRREPS + vsym[vb]
        n = tab[t.nk + row]

        @pl.loop(0, n)
        def _(rank, vb=vb, row=row, place0=total):
            place = place0 + rank

            def start(chunk, place0):
                pltpu.make_async_copy(
                    block(row, rank, vb), chunk.at[place - place0], sems.at[place]
                ).start()

            @pl.when(place < chunks[0])
            def _():
                start(packed[0], 0)

            @pl.when(place >= chunks[0])
            def _():
                place0 = chunks[0]
                for size, chunk in zip(chunks[1:], packed[1:]):

                    @pl.when((place >= place0) & (place < place0 + size))
                    def _(chunk=chunk, place0=place0):
                        start(chunk, place0)

                    place0 += size

        total = total + n

    vir = lax.axis_index("vir")
    step = min(width, BLK)
    copies = []
    for q in range(width // step):
        s = ksym[(vir * width + q * step) // BLK]
        cols = slice(q * step, (q + 1) * step)
        found = jnp.int32(0)
        slots = [jnp.int32(-1)] * MAXO
        for ob in range(oblocks):
            match = osym[ob] == s
            slots = [
                jnp.where(match & (found == i), ob, slot) for i, slot in enumerate(slots)
            ]
            found = found + match.astype(jnp.int32)
        for i, ob in enumerate(slots):
            copy = pltpu.make_async_copy(
                a_ref.at[
                    pl.ds(pl.multiple_of(jnp.maximum(ob, 0) * BLK, BLK), BLK),
                    pl.ds(q * step, step),
                ],
                pay.at[pl.ds(i * BLK, BLK), pl.ds(q * step, step)],
                pay_sems.at[q * MAXO + i],
            )
            copies.append((ob, copy))

            @pl.when(ob >= 0)
            def _(copy=copy):
                copy.start()

            @pl.when(ob < 0)
            def _(i=i, cols=cols):
                pay[i * BLK : (i + 1) * BLK, cols] = jnp.zeros((BLK, step), jnp.bfloat16)

    contraction_lists(t, ksym, tab, others)
    most = total
    for half in others:
        other = jnp.int32(0)
        for vb in range(vblocks):
            other = other + tab[t.nk + half * IRREPS + vsym[vb]]
        most = jnp.maximum(most, other)

    pay[MAXO * BLK :, :] = jnp.full(
        (INFO, width), most.astype(jnp.float32), jnp.float32
    ).astype(jnp.bfloat16)

    for ob, copy in copies:

        @pl.when(ob >= 0)
        def _(copy=copy):
            copy.wait()

    @pl.loop(0, total)
    def _(place):
        pltpu.make_async_copy(
            v_ref.at[pl.ds(0, BLK), pl.ds(0, BLK)], packed[0].at[0], sems.at[place]
        ).wait()


def plan_kernel(t, ksym, vsym, osym, after, out, tab, *refs):
    del after
    zeros, sems = refs[-2:]
    zeros[...] = jnp.zeros_like(zeros)
    fills = [
        pltpu.make_async_copy(zeros, out.at[pl.ds(i * BLK, BLK)], sems.at[i])
        for i in range(out.shape[0] // BLK)
    ]
    for fill in fills:
        fill.start()

    contraction_lists(t, ksym, tab, range(t.n_occ))
    for s in range(IRREPS):
        tab[t.cnt + s] = 0
        for slot in range(MAXO):
            tab[t.slot + s * MAXO + slot] = -1
    for ob in range(osym.shape[0]):
        s = osym[ob]
        used = (tab[t.slot + s * MAXO] >= 0).astype(jnp.int32)
        tab[t.slot + s * MAXO + used] = ob

    def count(vb, places):
        s = vsym[vb]
        rank = tab[t.cnt + s]
        tab[t.vbl + s * MAXB + rank] = vb
        tab[t.cnt + s] = rank + 1
        new = []
        for half, place in enumerate(places):
            tab[t.off + half * t.vblocks + vb] = place
            new.append(place + tab[t.nk + half * IRREPS + s])
        return tuple(new)

    totals = lax.fori_loop(0, t.vblocks, count, (jnp.int32(0),) * t.n_occ)
    for half, total in enumerate(totals):
        tab[t.total + half] = total
    tab[t.active] = 0
    for slots in range(MAXO, 0, -1):
        for s in range(IRREPS):
            fit = tab[t.slot + s * MAXO + slots - 1] >= 0
            if slots < MAXO:
                fit = fit & (tab[t.slot + s * MAXO + slots] < 0)

            @pl.when((tab[t.cnt + s] > 0) & fit)
            def _(s=s):
                used = tab[t.active]
                tab[t.active + 1 + used] = s
                tab[t.active] = used + 1
    for fill in fills:
        fill.wait()


def each_irrep(t, tab, act, variants):
    @pl.loop(0, tab[t.active])
    def _(i):
        s = tab[t.active + 1 + i]
        count = tab[t.cnt + s]
        rows = jnp.int32(BLK)
        for slot in range(1, MAXO):
            more = tab[t.slot + s * MAXO + slot] >= 0
            rows = jnp.where(more, (slot + 1) * BLK, rows)
        todo = count > 0
        for have, width in variants:
            fits = todo & (rows <= have) & (count <= width)

            @pl.when(fits)
            def _():
                act(
                    s,
                    have,
                    [
                        jnp.where(j < count, tab[t.vbl + s * MAXB + j], -1)
                        for j in range(width)
                    ],
                )

            todo = todo & jnp.logical_not(fits)


def multiply(t, tab, halves, s, rows, vbs, amp, sources, acc):
    bases = [half * IRREPS + s for half in halves]
    counts = [tab[t.nk + row] for row in bases]
    offs = [
        [jnp.where(vb >= 0, tab[t.off + half * t.vblocks + jnp.maximum(vb, 0)], 0) for vb in vbs]
        for half in halves
    ]
    steps = counts[0]
    for count in counts[1:]:
        steps = jnp.maximum(steps, count)

    def terms(rank):
        lefts, rights = [], [[] for _ in vbs]
        for row, count, places, source in zip(bases, counts, offs, sources):
            there = rank < count
            here = jnp.where(there, rank, 0)
            kb = jnp.where(there, tab[t.kbl + row * t.own + here], 0)
            left = amp[kb, :rows, :]
            lefts.append(jnp.where(there, left, jnp.zeros_like(left)))
            for place, column in zip(places, rights):
                right = source[jnp.where(there, place + here, 0)]
                column.append(jnp.where(there, right, jnp.zeros_like(right)))
        left = jnp.concatenate(lefts, axis=1)
        return [
            jnp.dot(
                left,
                jnp.concatenate(column, axis=0),
                preferred_element_type=jnp.float32,
            )
            for column in rights
        ]

    for j, part in enumerate(terms(jnp.int32(0))):
        acc[j, :rows, :] = part

    @pl.loop(1, steps)
    def _(rank):
        for j, part in enumerate(terms(rank)):
            acc[j, :rows, :] += part


def sort_kernel(masks, *refs):
    parts, (amp, most) = refs[:-2], refs[-2:]
    peak = parts[0][..., MAXO * BLK :, :].astype(jnp.float32)
    if masks:
        me = lax.axis_index("vir")
        for mask, part in zip(masks, parts):
            amp[me ^ mask] = part[: MAXO * BLK, :]
            peak = jnp.maximum(peak, part[MAXO * BLK :, :].astype(jnp.float32))
    else:
        amp[...] = parts[0][:, : MAXO * BLK, :]
    most[0] = jnp.max(peak).astype(jnp.int32)


def finish_kernel(t, chunks, tab, amp, *refs):
    n = t.n_occ
    heads, rests = refs[:n], refs[n : n * len(chunks)]
    _, out, acc, stage, blocks, sent, sems, load_sems = refs[n * len(chunks) :]
    me = lax.axis_index("occ")
    halves = [lax.rem(me - shift + n, n) for shift in range(n)]

    sent[0] = 0

    def send(s, slot, vb, index):
        ob = tab[t.slot + s * MAXO + slot]
        return pltpu.make_async_copy(
            stage.at[vb, pl.ds(slot * BLK, BLK)],
            out.at[
                pl.ds(pl.multiple_of(ob * BLK, BLK), BLK),
                pl.ds(pl.multiple_of(vb * BLK, BLK), BLK),
            ],
            sems.at[index],
        )

    def store(s, slot, j, vb):
        rows = slice(slot * BLK, (slot + 1) * BLK)
        stage[vb, rows, :] = acc[j, rows, :].astype(jnp.bfloat16)
        index = sent[0]
        send(s, slot, vb, index).start()
        sent[0] = index + 1

    def products(sources, variants):
        def act(s, rows, vbs):
            multiply(t, tab, halves, s, rows, vbs, amp, sources, acc)
            for j, vb in enumerate(vbs):
                for slot in range(rows // BLK):

                    @pl.when((vb >= 0) & (tab[t.slot + s * MAXO + slot] >= 0))
                    def _():
                        store(s, slot, j, vb)

        each_irrep(t, tab, act, variants)

    whole = ((MAXO * BLK, MAXB),)
    usual = ((BLK, 2), (BLK, 3), (BLK, MAXB), (MAXO * BLK, 3)) + whole

    most = tab[t.total]
    for half in range(1, n):
        most = jnp.maximum(most, tab[t.total + half])

    @pl.when(most <= chunks[0])
    def _():
        products(heads, usual)

    @pl.when(most > chunks[0])
    def _():
        def load(act):
            place = chunks[0]
            for c, size in enumerate(chunks[1:]):

                @pl.when(most > place)
                def _(c=c, size=size, place=place):
                    for i in range(n):
                        act(
                            pltpu.make_async_copy(
                                rests[c * n + i],
                                blocks.at[i, pl.ds(place, size)],
                                load_sems.at[c * n + i],
                            )
                        )

                place += size

        load(lambda copy: copy.start())
        for i in range(n):
            blocks[i, : chunks[0]] = heads[i][...]
        load(lambda copy: copy.wait())
        products([blocks.at[i] for i in range(n)], usual)

    @pl.loop(0, sent[0])
    def _(index):
        pltpu.make_async_copy(
            stage.at[0, pl.ds(0, BLK)],
            out.at[pl.ds(0, BLK), pl.ds(0, BLK)],
            sems.at[index],
        ).wait()


def per_device(n_occ, n_vir, amplitudes, integrals, occ_sym, vir_sym, k_sym):
    occ_rows, width = amplitudes.shape
    kblocks = k_sym.shape[0]
    vblocks = vir_sym.shape[0]
    cols = vblocks * BLK
    t = Table(n_occ, kblocks, vblocks)
    cap = t.own * MAXB
    first_cap = (cap * 28 + 39) // 40
    more_cap = (cap - first_cap) // 3
    chunks = tuple(c for c in (first_cap, more_cap, cap - first_cap - more_cap) if c)
    rows = MAXO * BLK + INFO
    bf16, f32, i32 = jnp.bfloat16, jnp.float32, jnp.int32

    *packed, pay = pl.pallas_call(
        functools.partial(pack_kernel, t, chunks),
        out_shape=tuple(pltpu.VMEM((c, BLK, BLK), bf16) for c in chunks)
        + (pltpu.VMEM((rows, width), bf16),),
        in_specs=[SMEM, SMEM, SMEM, HBM, HBM],
        out_specs=(VMEM,) * (len(chunks) + 1),
        scratch_shapes=[
            pltpu.SMEM((t.size,), i32),
            pltpu.SemaphoreType.DMA((cap,)),
            pltpu.SemaphoreType.DMA((MAXO * max(width // BLK, 1),)),
        ],
        compiler_params=pltpu.CompilerParams(vmem_limit_bytes=8 * 2**20),
        name="pack",
    )(*[away(x) for x in (k_sym, vir_sym, occ_sym, integrals, amplitudes)])
    zero_out, tab, *spares = pl.pallas_call(
        functools.partial(plan_kernel, t),
        out_shape=(pltpu.HBM((occ_rows, cols), bf16), pltpu.SMEM((t.size,), i32))
        + tuple(
            pltpu.HBM((c, BLK, BLK), bf16) for c in chunks[1:] for _ in range(n_occ - 1)
        ),
        in_specs=[SMEM, SMEM, SMEM, ANY],
        out_specs=(HBM, SMEM) + (HBM,) * ((n_occ - 1) * (len(chunks) - 1)),
        scratch_shapes=[
            pltpu.VMEM((BLK, cols), bf16),
            pltpu.SemaphoreType.DMA((occ_rows // BLK,)),
        ],
        compiler_params=pltpu.CompilerParams(vmem_limit_bytes=4 * 2**20),
        name="plan",
    )(*[away(x) for x in (k_sym, vir_sym, occ_sym)], pay)

    shifts = tuple(range(1, n_occ))

    def across(x, shift):
        return lax.ppermute(x, "occ", [(i, (i + shift) % n_occ) for i in range(n_occ)])

    heads = [across(packed[0], shift) for shift in shifts]

    bits = [1 << b for b in range(n_vir.bit_length() - 1)][::-1]
    masks = [0]
    for bit in bits:
        masks = masks + [m ^ bit for m in masks]
    if width == BLK:
        parts = [pay]
        for bit in bits:
            pairs = [(i, i ^ bit) for i in range(n_vir)]
            parts = parts + [lax.ppermute(p, "vir", pairs) for p in parts]
            if len(parts) == 8:
                parts[5], zero_out = lax.optimization_barrier((parts[5], zero_out))
    else:
        whole = pay[None]
        for bit in bits:
            pairs = [(i, i ^ bit) for i in range(n_vir)]
            whole = jnp.concatenate([whole, lax.ppermute(whole, "vir", pairs)])
        place = [masks.index(m) for m in range(n_vir)]
        order = jnp.asarray(place, i32)[
            jnp.arange(n_vir, dtype=i32) ^ lax.axis_index("vir").astype(i32)
        ]
        whole = whole[order].transpose(1, 0, 2).reshape(rows, kblocks, BLK)
        parts, masks = [whole.transpose(1, 0, 2)], []

    amp, most = pl.pallas_call(
        functools.partial(sort_kernel, tuple(masks)),
        out_shape=(
            pltpu.VMEM((kblocks, MAXO * BLK, BLK), bf16),
            jax.ShapeDtypeStruct((1,), i32),
        ),
        in_specs=[VMEM] * len(parts),
        out_specs=(VMEM, SMEM),
        compiler_params=pltpu.CompilerParams(vmem_limit_bytes=8 * 2**20),
        name="sort",
    )(*parts)

    n = len(shifts)
    spares = [spares[c * n : (c + 1) * n] for c in range(len(chunks) - 1)]

    def more(level, place, operands):
        if level == len(chunks):
            return []
        return lax.cond(
            most[0] > place,
            lambda packed, spares: [[across(packed[0], shift) for shift in shifts]]
            + more(level + 1, place + chunks[level], (packed[1:], spares[1:])),
            lambda packed, spares: list(spares),
            *operands,
        )

    rests = more(1, first_cap, (packed[1:], spares))
    heads = [packed[0]] + heads
    rests = [x for own, others in zip(packed[1:], rests) for x in [own, *others]]
    return pl.pallas_call(
        functools.partial(finish_kernel, t, chunks),
        out_shape=jax.ShapeDtypeStruct((occ_rows, cols), bf16),
        in_specs=[SMEM] + [VMEM] * (1 + n_occ) + [ANY] * len(rests) + [HBM],
        out_specs=HBM,
        scratch_shapes=[
            pltpu.VMEM((MAXB, MAXO * BLK, BLK), f32),
            pltpu.VMEM((vblocks, MAXO * BLK, BLK), bf16),
            pltpu.VMEM((n_occ, cap, BLK, BLK), bf16),
            pltpu.SMEM((1,), i32),
            pltpu.SemaphoreType.DMA((vblocks * MAXO,)),
            pltpu.SemaphoreType.DMA((max(len(rests), 1),)),
        ],
        input_output_aliases={2 + n_occ + len(rests): 0},
        compiler_params=pltpu.CompilerParams(vmem_limit_bytes=24 * 2**20),
        name="finish",
    )(tab, *[here(x) for x in (amp, *heads)], *rests, zero_out)


def solution(mesh):
    return jax.shard_map(
        functools.partial(per_device, mesh.shape["occ"], mesh.shape["vir"]),
        mesh=mesh,
        in_specs=(P("occ", "vir"), P("occ", "vir"), P("occ"), P("vir"), P()),
        out_specs=P("occ", "vir"),
        check_vma=False,
    )
```
